128 devices in a mesh: gx: 4 (over y), gy: 32 (over z, x, core).
Axes of the slice: x: 4, y: 4, z: 4, core: 2. Of those that a mesh axis runs over, the one named last changes fastest.
Arguments:
- features: float32 [7, 1048576], P(None, ('gx', 'gy')), may hold values from -4 to 4
- first_slot: int32 [4096], P(('gx', 'gy')), may hold values from 0 to 7
- second_owner: int32 [4096, 1], P(('gx', 'gy')), may hold values from 0 to 31; in each aligned block of 32 rows (0 to 31, 32 to 63, ...) at most 2 rows name the same one
- second_slot: int32 [4096], P(('gx', 'gy')), may hold values from 0 to 7
- pair_count: int32 [128], P(('gx', 'gy')), may hold values from 1 to 32, as said below
Outputs:
- gradient: float32 [6, 1048576], P(None, ('gx', 'gy'))
- energy: float32 [], replicated
The draws below stay inside these ranges and needn't reach their ends.
Inputs may be any that keep to these rules, and one draw needn't show every extreme that they name: `pair_count`: some device holds exactly 32 live entries. `second_owner`: among the 32 entries of one device, live or not, at most 2 name the same owner; in some devices one owner is named exactly 2 times.
All inputs are finite; a program needn't handle non-finite values.
Results may differ from the reference program's by a relative error of at most 0.0003.
Values sent between devices are 32-bit elements; how exact they have to be, the bound alone decides.
A program may use at most 64 MiB of HBM per device.

```python
import math
import jax
import jax.numpy as jnp
import numpy as np
from jax import lax

BLOCK = 1024
BLK_DEV = 8
PAIRS_DEV = 32
GROUP = 32
CAP = 2
BLOCKS = 1024
TRIANGLES = 1048576
PAIRS = 4096
DEVICES = 128


def draw_features(key, part):
    key = jax.random.fold_in(key, 17)
    keys = jax.random.split(key, 3)
    centers = jax.random.uniform(keys[0], (3, TRIANGLES), jnp.float32, -3.8, 3.8)
    normals = jnp.clip(0.7 * jax.random.normal(keys[1], (3, TRIANGLES), jnp.float32), -4.0, 4.0)
    masses = jnp.clip(0.7 * jax.random.normal(keys[2], (1, TRIANGLES), jnp.float32), -4.0, 4.0)
    return jnp.concatenate([centers, normals, masses], axis=0).astype(jnp.float32)


def draw_pair_count(key, part):
    keys = jax.random.split(key, 4)
    base = jax.random.randint(keys[0], (DEVICES,), PAIRS_DEV // 2, PAIRS_DEV + 1)
    busy = jax.random.randint(keys[1], (DEVICES,), 0, 8) == 0
    heavy = jax.random.randint(keys[2], (DEVICES,), 3 * PAIRS_DEV // 4, PAIRS_DEV + 1)
    counts = jnp.where(busy, heavy, base)
    fullest = jax.random.randint(keys[3], (), 0, DEVICES)
    counts = counts.at[fullest].set(PAIRS_DEV)
    return counts.astype(jnp.int32)


def touch_ends(entries, key, low, high):
    place = [jax.random.randint(jax.random.fold_in(key, axis), (), 0, length) for axis, length in enumerate(entries.shape)]
    longest = entries.shape.index(max(entries.shape))
    beside = place[:longest] + [(place[longest] + 1) % entries.shape[longest]] + place[longest + 1:]
    return entries.at[tuple(place)].set(low).at[tuple(beside)].set(high)


def routed_block(stream_key, own, number, rows, count, top, reach, slope):
    order = jax.random.permutation(stream_key, count)
    crowded, ordinary = load_shares(count, rows * top, reach, slope, True), load_shares(count, rows * top, reach, slope, False)
    places = jnp.arange(count)

    def named(sizes, offset_by):
        used = int((sizes > 0).sum())
        fixed = max(1, used // 4)
        shifted = fixed + (places - fixed + offset_by * (used - fixed)) % max(1, count - fixed)
        return jnp.zeros((count,), jnp.int32).at[order[jnp.where(places < fixed, places, shifted)]].set(jnp.asarray(sizes, jnp.int32))

    sizes = jnp.where(number % 4 == 0, named(crowded, number // 4), named(ordinary, number - number // 4 - 1))
    mixed = jax.random.permutation(jax.random.fold_in(own, 3), count)
    donor, sink = mixed[0:count // 2 * 2:2], mixed[1:count // 2 * 2:2]
    room = jnp.minimum(sizes[donor] - 1, reach - sizes[sink]) // 2
    room = jnp.where((donor == order[0]) | (sink == order[0]) | (sizes[sink] == 0), 0, jnp.maximum(room, 0))
    shifted = jax.random.randint(jax.random.fold_in(own, 4), (count // 2,), 0, 1 << 20) % (room + 1)
    sizes = sizes.at[donor].add(-shifted).at[sink].add(shifted)
    members = jnp.searchsorted(jnp.cumsum(sizes), jnp.arange(rows * top), side="right").astype(jnp.int32)
    table = members.reshape(top, rows).T
    table = table[jax.random.permutation(jax.random.fold_in(own, 1), rows)]
    offset_by = jax.random.randint(jax.random.fold_in(own, 2), (rows, 1), 0, top)
    return jnp.take_along_axis(table, (jnp.arange(top)[None, :] + offset_by) % top, axis=1)


def load_shares(amount, total, reach, skew, full):
    weights = [(1 << 20) // math.isqrt(rank ** skew) + 1 for rank in range(1, amount + 1)]
    largest = reach if full else min(reach, max(-(-total // amount), total * weights[0] // sum(weights)))
    least = 1 if total - largest >= amount - 1 else 0
    given, surplus = [largest] + [least] * (amount - 1), total - largest - least * (amount - 1)
    while surplus > 0:
        free = [i for i in range(1, amount) if given[i] < largest] or [i for i in range(1, amount) if given[i] < reach]
        mass, left = sum([weights[i] for i in free]), surplus
        for i in free:
            extra = min(reach - given[i], max(1, left * weights[i] // mass), surplus)
            given[i] = given[i] + extra
            surplus = surplus - extra
    return np.array(given)


def setup_inputs(seed: int = 0) -> dict:
    splits = jax.random.split(jax.random.key(seed), 6)
    features = draw_features(jax.random.fold_in(splits[5], 71), 0)
    first_slot = touch_ends(jax.random.randint(splits[1], (PAIRS,), 0, BLK_DEV), jax.random.fold_in(splits[1], 1), 0, BLK_DEV - 1).astype(jnp.int32)
    second_owner_keys = jax.random.split(jax.random.fold_in(splits[2], 1), PAIRS // PAIRS_DEV)
    second_owner_turns = jax.random.permutation(jax.random.fold_in(splits[2], 3), PAIRS // PAIRS_DEV)
    second_owner = jax.vmap(lambda own, number: routed_block(jax.random.fold_in(splits[2], 2), own, number, PAIRS_DEV, GROUP, 1, CAP, 2))(second_owner_keys, second_owner_turns).reshape((PAIRS, 1))
    second_slot = touch_ends(jax.random.randint(splits[3], (PAIRS,), 0, BLK_DEV), jax.random.fold_in(splits[3], 1), 0, BLK_DEV - 1).astype(jnp.int32)
    pair_count = draw_pair_count(jax.random.fold_in(splits[5], 71), 0)
    return {"features": features, "first_slot": first_slot, "second_owner": second_owner, "second_slot": second_slot, "pair_count": pair_count}


def contract_cols(left, right):
    return lax.dot_general(left, right, (((1,), (1,)), ((), ())), precision=lax.Precision.HIGHEST, preferred_element_type=jnp.float32)


def contract_rows(left, right):
    return jnp.dot(left, right, precision=lax.Precision.HIGHEST, preferred_element_type=jnp.float32)


def tile_terms(first_block, second_block, factor):
    dist_sq = jnp.zeros((first_block.shape[1], second_block.shape[1]), jnp.float32)
    alignment = jnp.zeros((first_block.shape[1], second_block.shape[1]), jnp.float32)
    for coord in range(3):
        diff = first_block[coord][:, None] - second_block[coord][None, :]
        dist_sq = dist_sq + diff * diff
        alignment = alignment + first_block[3 + coord][:, None] * second_block[3 + coord][None, :]
    weights = first_block[6][:, None] * second_block[6][None, :]
    gaussian = jnp.exp(-0.5 * dist_sq)
    kernel = weights * gaussian * alignment * alignment
    energy = factor * jnp.sum(kernel)
    pulling = -factor * kernel
    turning = 2.0 * factor * weights * gaussian * alignment
    first_pos = first_block[0:3]
    second_pos = second_block[0:3]
    grad_first = jnp.concatenate([first_pos * jnp.sum(pulling, axis=1)[None, :] - contract_cols(second_pos, pulling), contract_cols(second_block[3:6], turning)], axis=0)
    grad_second = jnp.concatenate([second_pos * jnp.sum(pulling, axis=0)[None, :] - contract_rows(first_pos, pulling), contract_rows(first_block[3:6], turning)], axis=0)
    return grad_first, grad_second, energy


def reference(features, first_slot, second_owner, second_slot, pair_count):
    blocks = features.reshape(7, BLOCKS, BLOCK).transpose(1, 0, 2)
    gradients = jnp.zeros((BLOCKS, 6, BLOCK), jnp.float32)
    total = jnp.zeros((), jnp.float32)

    def visit_entry(carried, entry_index):
        device = entry_index // PAIRS_DEV
        active = (entry_index % PAIRS_DEV) < pair_count[device]
        first_block = device * BLK_DEV + first_slot[entry_index]
        second_block = ((device // GROUP) * GROUP + second_owner[entry_index, 0]) * BLK_DEV + second_slot[entry_index]
        factor = jnp.where(first_block == second_block, 1.0, 2.0).astype(jnp.float32)

        def work(state):
            grads_now, total_now = state
            grad_first, grad_second, energy = tile_terms(blocks[first_block], blocks[second_block], factor)
            grads_now = grads_now.at[first_block].add(grad_first)
            grads_now = grads_now.at[second_block].add(grad_second)
            return grads_now, total_now + energy

        return lax.cond(active, work, lambda state: state, carried), None

    (gradients, total), _ = lax.scan(visit_entry, (gradients, total), jnp.arange(PAIRS, dtype=jnp.int32))
    gradient = gradients.transpose(1, 0, 2).reshape(6, TRIANGLES)
    return gradient, total / BLOCK
```

```python
import jax
import jax.numpy as jnp
from jax import lax
from jax.experimental import pallas as pl
from jax.experimental.pallas import tpu as pltpu
from jax.sharding import PartitionSpec as P

BLOCK = 1024
TILE = 256
LOG2E = 1.4426950408889634
F32 = jnp.float32
BF16 = jnp.bfloat16


def dot(left, right, left_dim, right_dim):
    return lax.dot_general(
        left, right, (((left_dim,), (right_dim,)), ((), ())), preferred_element_type=F32
    )


def split_three(value):
    high = value.astype(BF16).astype(F32)
    rest = value - high
    mid = rest.astype(BF16).astype(F32)
    return high, mid, rest - mid


def select_rows(rows):
    index = lax.broadcasted_iota(jnp.int32, (8, BLOCK), 0)
    tile = jnp.zeros((8, BLOCK), F32)
    for place, row in enumerate(rows):
        tile = jnp.where(index == place, row, tile)
    return tile


def read_rows(block):
    return [block[row : row + 1] for row in range(7)]


def exponent_rows(rows):
    x, y, z = rows[:3]
    norm = (-0.5 * LOG2E) * (x * x + y * y + z * z)
    one = jnp.ones_like(x)
    left = select_rows([LOG2E * x, LOG2E * y, LOG2E * z, one, norm])
    right = select_rows([x, y, z, norm, one])
    return left, right


def left_splits(left):
    high, mid, low = split_three(left)
    return jnp.concatenate([high, high, mid, mid, high, low], axis=0)


def right_splits(right):
    high, mid, low = split_three(right)
    return jnp.concatenate([high, mid, high, mid, low, high], axis=0).astype(BF16)


def normal_products(rows):
    nx, ny, nz = rows[3:6]
    return select_rows([nx, ny, nz, nx, nx, ny]) * select_rows([nx, ny, nz, ny, nz, nz])


def moment_rows(rows):
    x, y, z, w = rows[0], rows[1], rows[2], rows[6]
    base = normal_products(rows) * w
    full = jnp.concatenate([base, base * x, base * y, base * z], axis=0)
    high = full.astype(BF16)
    low = (full - high.astype(F32)).astype(BF16)
    return jnp.concatenate([high, low], axis=0)


def finish(rows, moments, factor):
    x, y, z, nx, ny, nz, w = rows
    index = lax.broadcasted_iota(jnp.int32, (8, BLOCK), 0)
    doubled = normal_products(rows) * jnp.where(index < 3, 1.0, 2.0)
    mass = w * factor
    m0 = moments[0:8]
    sums = [
        jnp.sum(doubled * moments[8 * part : 8 * part + 8], axis=0, keepdims=True) * mass
        for part in range(4)
    ]
    xx, yy, zz, xy, xz, yz = [m0[row : row + 1] for row in range(6)]
    twice = 2.0 * mass
    out = select_rows(
        [
            sums[1] - x * sums[0],
            sums[2] - y * sums[0],
            sums[3] - z * sums[0],
            twice * (nx * xx + ny * xy + nz * xz),
            twice * (nx * xy + ny * yy + nz * yz),
            twice * (nx * xz + ny * yz + nz * zz),
        ]
    )
    return out, sums[0]


def pair_kernel(
    first_ref, slot_ref, same_ref, count_ref, features_ref, fetched_ref,
    local_ref, returned_ref, energy_ref, left_ref, moment_ref, total_ref,
):
    owned = left_ref.shape[0]
    total_ref[...] = jnp.zeros_like(total_ref)
    returned_ref[...] = jnp.zeros_like(returned_ref)

    def own_rows(block):
        start = pl.multiple_of(block * BLOCK, BLOCK)
        return read_rows(features_ref[:, pl.ds(start, BLOCK)])

    def prepare(block, carry):
        rows = own_rows(block)
        left, _ = exponent_rows(rows)
        left_ref[block] = left_splits(left).T.astype(BF16)
        moment_ref[block] = moment_rows(rows)
        return carry

    lax.fori_loop(0, owned, prepare, 0)

    def visit(entry, carry):
        block = first_ref[entry]
        slot = slot_ref[entry]
        factor = same_ref[entry]
        rows = read_rows(fetched_ref[slot])
        _, right = exponent_rows(rows)
        right = right_splits(right)
        second = moment_rows(rows)
        first = moment_ref[block]
        left = left_ref[block]

        def gaussians(tile):
            columns = slice(tile * TILE, (tile + 1) * TILE)
            value = jnp.exp2(dot(left, right[:, columns], 1, 0))
            high = value.astype(BF16)
            return high, (value - high.astype(F32)).astype(BF16)

        by_first = None
        by_second = []

        def contract(tile, high, low, by_first):
            columns = slice(tile * TILE, (tile + 1) * TILE)
            part = dot(high, second[:, columns], 1, 1) + dot(low, second[:, columns], 1, 1)
            by_first = part if by_first is None else by_first + part
            both = dot(first, high, 1, 0)
            by_second.append(both[0:32] + both[32:64] + dot(first[0:32], low, 1, 0))
            return by_first

        tiles = BLOCK // TILE
        held = gaussians(0)
        for tile in range(tiles):
            later = gaussians(tile + 1) if tile + 1 < tiles else None
            by_first = contract(tile, *held, by_first)
            held = later
        total_ref[block] += factor * by_first
        returned_ref[slot] = finish(rows, jnp.concatenate(by_second, axis=1), factor)[0][0:6]
        return carry

    lax.fori_loop(0, count_ref[0], visit, 0)

    def close(block, energy):
        rows = own_rows(block)
        both = total_ref[block].T
        out, share = finish(rows, both[0:32] + both[32:64], 1.0)
        start = pl.multiple_of(block * BLOCK, BLOCK)
        local_ref[:, pl.ds(start, BLOCK)] = out[0:6]
        return energy + share

    energy = lax.fori_loop(0, owned, close, jnp.zeros((1, BLOCK), F32))
    energy_ref[...] = energy


def shards(features, first_slot, second_owner, second_slot, pair_count):
    owned = features.shape[1] // BLOCK
    blocks = features.reshape(7, owned, BLOCK).transpose(1, 0, 2)
    entries = first_slot.shape[0]
    groups = lax.axis_size("gy")
    capacity = max(2, entries // groups)
    slots = groups * capacity
    self_index = lax.axis_index("gy")
    owners = second_owner[:, 0]
    live = jnp.arange(entries, dtype=jnp.int32) < pair_count[0]
    factors = jnp.where((owners == self_index) & (second_slot == first_slot), 1.0, 2.0).astype(F32)
    owner_hits = (owners[:, None] == jnp.arange(groups, dtype=jnp.int32)[None, :]) & live[:, None]
    running = jnp.cumsum(owner_hits.astype(jnp.int32), axis=0) - 1
    order_rank = jnp.sum(jnp.where(owner_hits, running, 0), axis=1)
    slot_index = owners * capacity + order_rank
    slot_table = (
        slot_index[:, None] == jnp.arange(slots, dtype=jnp.int32)[None, :]
    ) & live[:, None]
    wanted = jnp.sum(jnp.where(slot_table, second_slot[:, None] + 1, 0), axis=0) - 1
    requested = lax.all_to_all(
        wanted.reshape(groups, capacity), "gy", split_axis=0, concat_axis=0, tiled=True
    ).reshape(slots)
    outgoing = blocks[jnp.clip(requested, 0, owned - 1)]
    fetched = lax.all_to_all(
        outgoing.reshape(groups, capacity, 7, BLOCK), "gy", split_axis=0, concat_axis=0, tiled=True
    ).reshape(slots, 7, BLOCK)

    smem = pl.BlockSpec(memory_space=pltpu.SMEM)
    vmem = pl.BlockSpec(memory_space=pltpu.VMEM)
    local_grads, returned, energy_rows = pl.pallas_call(
        pair_kernel,
        out_shape=[
            jax.ShapeDtypeStruct((6, owned * BLOCK), F32),
            jax.ShapeDtypeStruct((slots, 6, BLOCK), F32),
            jax.ShapeDtypeStruct((1, BLOCK), F32),
        ],
        in_specs=[smem, smem, smem, smem, vmem, vmem],
        out_specs=[vmem, vmem, vmem],
        scratch_shapes=[
            pltpu.VMEM((owned, BLOCK, 48), BF16),
            pltpu.VMEM((owned, 64, BLOCK), BF16),
            pltpu.VMEM((owned, BLOCK, 64), F32),
        ],
        compiler_params=pltpu.CompilerParams(vmem_limit_bytes=48 * 2**20),
    )(first_slot, slot_index, factors, pair_count, features, fetched)

    arrived = lax.all_to_all(
        returned.reshape(groups, capacity, 6, BLOCK),
        "gy",
        split_axis=0,
        concat_axis=0,
        tiled=True,
    ).reshape(slots, 6, BLOCK)
    selector = (requested[:, None] == jnp.arange(owned, dtype=jnp.int32)[None, :]).astype(F32)
    remote = jnp.einsum("sl,sfb->flb", selector, arrived, precision=lax.Precision.HIGHEST)
    gradient = local_grads + remote.reshape(6, owned * BLOCK)
    total = lax.psum(jnp.sum(energy_rows), ("gx", "gy"))
    return (gradient, total / BLOCK)


def solution(mesh):
    return jax.shard_map(
        shards,
        mesh=mesh,
        in_specs=(
            P(None, ("gx", "gy")),
            P(("gx", "gy")),
            P(("gx", "gy"), None),
            P(("gx", "gy")),
            P(("gx", "gy")),
        ),
        out_specs=(P(None, ("gx", "gy")), P()),
        check_vma=False,
    )
```

```python
import jax
import jax.numpy as jnp
from jax import lax
from jax.experimental import pallas as pl
from jax.experimental.pallas import tpu as pltpu
from jax.sharding import PartitionSpec as P

BLOCK = 1024
TILE = 256
LOG2E = 1.4426950408889634
F32 = jnp.float32
BF16 = jnp.bfloat16


def dot(left, right, left_dim, right_dim):
    return lax.dot_general(
        left, right, (((left_dim,), (right_dim,)), ((), ())), preferred_element_type=F32
    )


def split_three(value):
    high = value.astype(BF16).astype(F32)
    rest = value - high
    mid = rest.astype(BF16).astype(F32)
    return high, mid, rest - mid


def select_rows(rows):
    index = lax.broadcasted_iota(jnp.int32, (8, BLOCK), 0)
    tile = jnp.zeros((8, BLOCK), F32)
    for place, row in enumerate(rows):
        tile = jnp.where(index == place, row, tile)
    return tile


def read_rows(block):
    return [block[row : row + 1] for row in range(7)]


def exponent_rows(rows):
    x, y, z = rows[:3]
    norm = (-0.5 * LOG2E) * (x * x + y * y + z * z)
    one = jnp.ones_like(x)
    left = select_rows([LOG2E * x, LOG2E * y, LOG2E * z, one, norm])
    right = select_rows([x, y, z, norm, one])
    return left, right


def left_splits(left):
    high, mid, low = split_three(left)
    return jnp.concatenate([high, high, mid, mid, high, low], axis=0)


def right_splits(right):
    high, mid, low = split_three(right)
    return jnp.concatenate([high, mid, high, mid, low, high], axis=0).astype(BF16)


def normal_products(rows):
    nx, ny, nz = rows[3:6]
    return select_rows([nx, ny, nz, nx, nx, ny]) * select_rows([nx, ny, nz, ny, nz, nz])


def moment_rows(rows):
    x, y, z, w = rows[0], rows[1], rows[2], rows[6]
    base = normal_products(rows) * w
    full = jnp.concatenate([base, base * x, base * y, base * z], axis=0)
    high = full.astype(BF16)
    low = (full - high.astype(F32)).astype(BF16)
    return jnp.concatenate([high, low], axis=0)


def finish(rows, moments, factor):
    x, y, z, nx, ny, nz, w = rows
    index = lax.broadcasted_iota(jnp.int32, (8, BLOCK), 0)
    doubled = normal_products(rows) * jnp.where(index < 3, 1.0, 2.0)
    mass = w * factor
    m0 = moments[0:8]
    sums = [
        jnp.sum(doubled * moments[8 * part : 8 * part + 8], axis=0, keepdims=True) * mass
        for part in range(4)
    ]
    xx, yy, zz, xy, xz, yz = [m0[row : row + 1] for row in range(6)]
    twice = 2.0 * mass
    out = select_rows(
        [
            sums[1] - x * sums[0],
            sums[2] - y * sums[0],
            sums[3] - z * sums[0],
            twice * (nx * xx + ny * xy + nz * xz),
            twice * (nx * xy + ny * yy + nz * yz),
            twice * (nx * xz + ny * yz + nz * zz),
        ]
    )
    return out, sums[0]


def pair_kernel(
    plan_ref, want_ref, features_ref,
    grad_ref, energy_ref,
    block_ref, left_ref, moment_ref, ask_ref, asked_ref, out_ref,
    near_ref, far_ref, twin_ref, now_ref, mine_ref, result_ref, back_ref, home_ref,
    share_ref, across_ref, along_ref, send_sem, recv_sem, local_sem,
):
    groups = want_ref.shape[0]
    rows_x = lax.axis_size("gx")
    owned = block_ref.shape[0]
    near = near_ref.shape[0]
    head = near - groups // 2
    me = lax.axis_index("gy")
    my_row = lax.axis_index("gx")

    def ahead(r):
        return {"gy": lax.rem(me + r, groups)}

    def behind(r):
        return {"gy": lax.rem(me + groups - r, groups)}

    def remote(kind, r, source, target, device):
        return pltpu.make_async_remote_copy(
            src_ref=source, dst_ref=target, send_sem=send_sem.at[kind, r], recv_sem=recv_sem.at[kind, r],
            device_id=device, device_id_type=pl.DeviceIdType.MESH,
        )

    def ask(r):
        return remote(0, r, want_ref.at[r], ask_ref.at[r], ahead(r))

    def fetch_near(r):
        return remote(1, r, out_ref.at[r], near_ref.at[r], behind(r))

    def fetch_far(r):
        return remote(1, r, out_ref.at[r], far_ref.at[r - near], behind(r))

    def fetch_twin(r):
        return remote(2, r, out_ref.at[groups + r], twin_ref.at[r], behind(r))

    def give_back(rank, r):
        return remote(3 + rank, r, back_ref.at[rank * groups + r], home_ref.at[rank * groups + r], ahead(r))

    def share_across(r):
        return remote(5, r, share_ref.at[0], across_ref.at[my_row], {"gx": lax.rem(my_row + r, rows_x)})

    def share_along(r):
        return remote(6, r, share_ref.at[1], along_ref.at[me], ahead(r))

    def arrive_across(r):
        source_row = lax.rem(my_row + rows_x - r, rows_x)
        remote(5, r, share_ref.at[0], across_ref.at[source_row], {"gx": source_row}).wait_recv()

    def arrive_along(r):
        source = lax.rem(me + groups - r, groups)
        remote(6, r, share_ref.at[1], along_ref.at[source], {"gy": source}).wait_recv()

    def each(first, last, body):
        def step(r, carry):
            body(r)
            return carry

        lax.fori_loop(first, last, step, 0)

    barrier = pltpu.get_barrier_semaphore()

    def greet(r):
        pl.semaphore_signal(barrier, inc=1, device_id=ahead(r), device_id_type=pl.DeviceIdType.MESH)

    def greet_across(r):
        pl.semaphore_signal(
            barrier, inc=1, device_id={"gx": lax.rem(my_row + r, rows_x)}, device_id_type=pl.DeviceIdType.MESH
        )

    each(1, groups, greet)
    each(1, rows_x, greet_across)
    for block in range(owned):
        block_ref[block] = features_ref[:, block * BLOCK : (block + 1) * BLOCK]
    pl.semaphore_wait(barrier, groups - 1 + rows_x - 1)

    each(1, groups, lambda r: ask(r).start())
    ask_ref[0] = want_ref[0]
    each(1, groups, lambda r: ask(r).wait_recv())
    fetch_plan = pltpu.make_async_copy(ask_ref, asked_ref, local_sem)
    fetch_plan.start()
    fetch_plan.wait()

    def load_out(place, r):
        out_ref[place * groups + r] = block_ref[jnp.maximum(asked_ref[r, 0, place], 0)]

    def send_near(r):
        load_out(0, r)
        fetch_near(r).start()

    def send_far(r):
        load_out(0, r)
        fetch_far(r).start()

    def send_twin(r):
        load_out(1, r)
        fetch_twin(r).start()

    each(1, near, send_near)
    each(near, groups, send_far)
    each(1, groups, send_twin)
    near_ref[0] = block_ref[jnp.maximum(asked_ref[0, 0, 0], 0)]
    twin_ref[0] = block_ref[jnp.maximum(asked_ref[0, 0, 1], 0)]

    def prepare(block):
        rows = read_rows(block_ref[block])
        left, _ = exponent_rows(rows)
        left_ref[block] = left_splits(left).T.astype(BF16)
        moment_ref[block] = moment_rows(rows)

    each(0, owned, prepare)
    result_ref[groups] = jnp.zeros_like(result_ref[groups])
    each(1, near, lambda r: fetch_near(r).wait_recv())

    def visit(step, energy):
        @pl.when(step == head)
        def _():
            each(near, groups, lambda r: fetch_far(r).wait_recv())

        @pl.when(step == groups // 2)
        def _():
            each(1, groups, lambda r: fetch_twin(r).wait_recv())

        block = plan_ref[step]
        key = plan_ref[groups + step]
        factor = plan_ref[6 * groups + step].astype(F32)
        now_ref[...] = near_ref[jnp.minimum(key, near - 1)]

        @pl.when(step >= head)
        def _():
            far_block = far_ref[jnp.clip(key - near, 0, groups - near - 1)]
            now_ref[...] = jnp.where(key >= near, far_block, now_ref[...])

        @pl.when(step >= groups // 2)
        def _():
            twin_block = twin_ref[jnp.maximum(key - groups, 0)]
            now_ref[...] = jnp.where(key >= groups, twin_block, now_ref[...])

        rows = read_rows(now_ref[...])
        _, right = exponent_rows(rows)
        right = right_splits(right)
        second = moment_rows(rows)
        first = moment_ref[block]
        left = left_ref[block]

        def gaussians(tile):
            columns = slice(tile * TILE, (tile + 1) * TILE)
            value = jnp.exp2(dot(left, right[:, columns], 1, 0))
            high = value.astype(BF16)
            return high, (value - high.astype(F32)).astype(BF16)

        by_first = None
        by_second = []

        def contract(tile, high, low, by_first):
            columns = slice(tile * TILE, (tile + 1) * TILE)
            both = dot(second[:, columns], high, 1, 1)
            part = both[0:32] + both[32:64] + dot(second[0:32, columns], low, 1, 1)
            by_first = part if by_first is None else by_first + part
            both = dot(first, high, 1, 0)
            by_second.append(both[0:32] + both[32:64] + dot(first[0:32], low, 1, 0))
            return by_first

        tiles = BLOCK // TILE
        held = gaussians(0)
        for tile in range(tiles):
            later = gaussians(tile + 1) if tile + 1 < tiles else None
            by_first = contract(tile, *held, by_first)
            held = later
        mine_ref[step] = by_first
        out, share = finish(rows, jnp.concatenate(by_second, axis=1), factor)
        result_ref[step] = out[0:6]
        back_ref[step] = result_ref[plan_ref[2 * groups + step]]

        @pl.when(step >= 1)
        def _():
            give_back(0, step).start()

        return energy + share

    energy = lax.fori_loop(0, groups, visit, jnp.zeros((1, BLOCK), F32))
    share_ref[0] = jnp.full(share_ref.shape[1:], jnp.sum(energy) * (1.0 / BLOCK), F32)
    each(1, rows_x, lambda r: share_across(r).start())

    def send_last(r):
        back_ref[groups + r] = result_ref[plan_ref[3 * groups + r]]
        give_back(1, r).start()

    each(1, groups, send_last)
    back_ref[groups] = result_ref[plan_ref[3 * groups]]
    home_ref[0] = back_ref[0]
    home_ref[groups] = back_ref[groups]

    def close(block):
        def add(step, moments):
            weight = jnp.where(plan_ref[step] == block, plan_ref[6 * groups + step], 0).astype(F32)
            return moments + weight * mine_ref[step]

        moments = lax.fori_loop(0, groups, add, jnp.zeros((32, BLOCK), F32))
        out, _ = finish(read_rows(block_ref[block]), moments, 1.0)
        grad_ref[:, pl.ds(pl.multiple_of(block * BLOCK, BLOCK), BLOCK)] = out[0:6]

    each(0, 1, close)
    across_ref[my_row] = share_ref[0]
    each(1, rows_x, lambda r: share_across(r).wait_send())
    each(1, rows_x, arrive_across)
    total = across_ref[0]
    for r in range(1, rows_x):
        total = total + across_ref[r]
    share_ref[1] = total
    each(1, groups, lambda r: share_along(r).start())
    along_ref[me] = total
    each(1, owned, close)

    each(1, groups, lambda r: give_back(0, r).wait_recv())
    each(1, groups, lambda r: give_back(1, r).wait_recv())

    width = TILE
    for start in range(0, BLOCK, width):
        def gather(slot, sums, start=start):
            piece = home_ref[slot, :, start : start + width]
            wish = asked_ref[lax.rem(slot, groups), 0, slot // groups]
            return tuple(
                kept + jnp.where(wish == block, piece, 0.0) for block, kept in enumerate(sums)
            )

        sums = lax.fori_loop(0, 2 * groups, gather, (jnp.zeros((6, width), F32),) * owned)
        for block in range(owned):
            grad_ref[:, block * BLOCK + start : block * BLOCK + start + width] += sums[block]

    each(1, groups, arrive_along)
    energy_ref[...] = lax.fori_loop(1, groups, lambda r, kept: kept + along_ref[r], along_ref[0])

    def drain(r):
        ask(r).wait_send()
        fetch_twin(r).wait_send()
        give_back(0, r).wait_send()
        give_back(1, r).wait_send()
        share_along(r).wait_send()

    each(1, groups, drain)
    each(1, near, lambda r: fetch_near(r).wait_send())
    each(near, groups, lambda r: fetch_far(r).wait_send())


def shards(features, first_slot, second_owner, second_slot, pair_count):
    owned = features.shape[1] // BLOCK
    entries = first_slot.shape[0]
    groups = lax.axis_size("gy")
    slots = 2 * groups
    near = groups // 2 + groups // 8
    me = lax.axis_index("gy")
    owners = second_owner[:, 0]
    order = jnp.arange(entries, dtype=jnp.int32)
    far = jnp.arange(slots, dtype=jnp.int32)
    live = order < pair_count[0]
    factors = jnp.where((owners == me) & (second_slot == first_slot), 1, 2)
    factors = jnp.where(live, factors, 0)
    rank = jnp.sum((owners[:, None] == owners[None, :]) & (order[None, :] < order[:, None]), axis=1)
    key = rank.astype(jnp.int32) * groups + lax.rem(owners - me + groups, groups)
    place = jnp.sum(key[None, :] < key[:, None], axis=1).astype(jnp.int32)
    at_step = place[None, :] == order[:, None]
    at_slot = key[None, :] == far[:, None]

    def pick(table, values):
        return jnp.sum(jnp.where(table, values[None, :], 0), axis=1)

    want = pick(at_slot, second_slot + 1) - 1
    serve = pick(at_slot, place - groups) + groups
    plan = jnp.concatenate(
        [pick(at_step, first_slot), pick(at_step, key), serve, want, pick(at_step, factors)]
    ).astype(jnp.int32)
    lane = jnp.arange(128, dtype=jnp.int32)[None, :]
    asked = jnp.where(lane == 0, want[:groups, None], jnp.where(lane == 1, want[groups:, None], 0))

    smem = pl.BlockSpec(memory_space=pltpu.SMEM)
    vmem = pl.BlockSpec(memory_space=pltpu.VMEM)
    gradient, energy = pl.pallas_call(
        pair_kernel,
        out_shape=[
            jax.ShapeDtypeStruct((6, owned * BLOCK), F32),
            jax.ShapeDtypeStruct((8, 128), F32),
        ],
        in_specs=[smem, vmem, vmem],
        out_specs=[vmem, vmem],
        scratch_shapes=[
            pltpu.VMEM((owned, 7, BLOCK), F32),
            pltpu.VMEM((owned, BLOCK, 48), BF16),
            pltpu.VMEM((owned, 64, BLOCK), BF16),
            pltpu.VMEM((groups, 1, 128), jnp.int32),
            pltpu.SMEM((groups, 1, 128), jnp.int32),
            pltpu.VMEM((slots, 7, BLOCK), F32),
            pltpu.VMEM((near, 7, BLOCK), F32),
            pltpu.VMEM((groups - near, 7, BLOCK), F32),
            pltpu.VMEM((groups, 7, BLOCK), F32),
            pltpu.VMEM((7, BLOCK), F32),
            pltpu.VMEM((groups, 32, BLOCK), F32),
            pltpu.VMEM((groups + 1, 6, BLOCK), F32),
            pltpu.VMEM((slots, 6, BLOCK), F32),
            pltpu.VMEM((slots, 6, BLOCK), F32),
            pltpu.VMEM((2, 8, 128), F32),
            pltpu.VMEM((lax.axis_size("gx"), 8, 128), F32),
            pltpu.VMEM((groups, 8, 128), F32),
            pltpu.SemaphoreType.DMA((7, groups)),
            pltpu.SemaphoreType.DMA((7, groups)),
            pltpu.SemaphoreType.DMA,
        ],
        compiler_params=pltpu.CompilerParams(
            vmem_limit_bytes=56 * 2**20, collective_id=0, has_side_effects=True
        ),
    )(plan, asked.reshape(groups, 1, 128), features)
    return (gradient, energy[0, 0])


def solution(mesh):
    return jax.shard_map(
        shards,
        mesh=mesh,
        in_specs=(
            P(None, ("gx", "gy")),
            P(("gx", "gy")),
            P(("gx", "gy"), None),
            P(("gx", "gy")),
            P(("gx", "gy")),
        ),
        out_specs=(P(None, ("gx", "gy")), P()),
        check_vma=False,
    )
```

```python
import jax
import jax.numpy as jnp
from jax import lax
from jax.experimental import pallas as pl
from jax.experimental.pallas import tpu as pltpu
from jax.sharding import PartitionSpec as P

BLOCK = 1024
TILE = 256
LOG2E = 1.4426950408889634
F32 = jnp.float32
BF16 = jnp.bfloat16


def dot(left, right, left_dim, right_dim):
    return lax.dot_general(
        left, right, (((left_dim,), (right_dim,)), ((), ())), preferred_element_type=F32
    )


def split_three(value):
    high = value.astype(BF16).astype(F32)
    rest = value - high
    mid = rest.astype(BF16).astype(F32)
    return high, mid, rest - mid


def select_rows(rows):
    index = lax.broadcasted_iota(jnp.int32, (8, BLOCK), 0)
    tile = jnp.zeros((8, BLOCK), F32)
    for place, row in enumerate(rows):
        tile = jnp.where(index == place, row, tile)
    return tile


def read_rows(block):
    return [block[row : row + 1] for row in range(7)]


def exponent_rows(rows):
    x, y, z = rows[:3]
    norm = (-0.5 * LOG2E) * (x * x + y * y + z * z)
    one = jnp.ones_like(x)
    left = select_rows([LOG2E * x, LOG2E * y, LOG2E * z, one, norm])
    right = select_rows([x, y, z, norm, one])
    return left, right


def left_splits(left):
    high, mid, low = split_three(left)
    return jnp.concatenate([high, high, mid, mid, high, low], axis=0)


def right_splits(right):
    high, mid, low = split_three(right)
    return jnp.concatenate([high, mid, high, mid, low, high], axis=0).astype(BF16)


def normal_products(rows):
    nx, ny, nz = rows[3:6]
    return select_rows([nx, ny, nz, nx, nx, ny]) * select_rows([nx, ny, nz, ny, nz, nz])


def moment_rows(rows):
    x, y, z, w = rows[0], rows[1], rows[2], rows[6]
    base = normal_products(rows) * w
    full = jnp.concatenate([base, base * x, base * y, base * z], axis=0)
    high = full.astype(BF16)
    low = (full - high.astype(F32)).astype(BF16)
    return jnp.concatenate([high, low], axis=0)


def finish(rows, moments, factor):
    x, y, z, nx, ny, nz, w = rows
    index = lax.broadcasted_iota(jnp.int32, (8, BLOCK), 0)
    doubled = normal_products(rows) * jnp.where(index < 3, 1.0, 2.0)
    mass = w * factor
    m0 = moments[0:8]
    sums = [
        jnp.sum(doubled * moments[8 * part : 8 * part + 8], axis=0, keepdims=True) * mass
        for part in range(4)
    ]
    xx, yy, zz, xy, xz, yz = [m0[row : row + 1] for row in range(6)]
    twice = 2.0 * mass
    out = select_rows(
        [
            sums[1] - x * sums[0],
            sums[2] - y * sums[0],
            sums[3] - z * sums[0],
            twice * (nx * xx + ny * xy + nz * xz),
            twice * (nx * xy + ny * yy + nz * yz),
            twice * (nx * xz + ny * yz + nz * zz),
        ]
    )
    return out, sums[0]


def pair_kernel(
    plan_ref, want_ref, features_ref,
    grad_ref, energy_ref,
    block_ref, left_ref, moment_ref, ask_ref, asked_ref, out_ref,
    near_ref, far_ref, twin_ref, now_ref, mine_ref, result_ref, back_ref, home_ref,
    share_ref, across_ref, along_ref, send_sem, recv_sem, local_sem,
):
    groups = want_ref.shape[0]
    rows_x = lax.axis_size("gx")
    owned = block_ref.shape[0]
    near = near_ref.shape[0]
    head = near - groups // 2
    me = lax.axis_index("gy")
    my_row = lax.axis_index("gx")

    def offset(r):
        half, odd = (r + 1) // 2, lax.rem(r, 2)
        return odd * half + (1 - odd) * (groups - half)

    def ahead(r):
        return {"gy": lax.rem(me + offset(r), groups)}

    def behind(r):
        return {"gy": lax.rem(me + 2 * groups - offset(r), groups)}

    def remote(kind, source, target, device):
        return pltpu.make_async_remote_copy(
            src_ref=source, dst_ref=target, send_sem=send_sem.at[kind], recv_sem=recv_sem.at[kind],
            device_id=device, device_id_type=pl.DeviceIdType.MESH,
        )

    def all_of(kind, source, target):
        return remote(kind, source, target, ahead(1))

    def ask(r):
        return remote(0, want_ref.at[r], ask_ref.at[r], ahead(r))

    def fetch_near(r):
        return remote(1, out_ref.at[r], near_ref.at[r], behind(r))

    def fetch_far(r):
        return remote(2, out_ref.at[r], far_ref.at[r - near], behind(r))

    def fetch_twin(r):
        return remote(3, out_ref.at[groups + r], twin_ref.at[r], behind(r))

    def give_back(rank, r):
        return remote(4 + rank, back_ref.at[rank * groups + r], home_ref.at[rank * groups + r], ahead(r))

    def share_across(r):
        return remote(6, share_ref.at[0], across_ref.at[my_row], {"gx": lax.rem(my_row + r, rows_x)})

    def share_along(r):
        return remote(7, share_ref.at[1], along_ref.at[me], ahead(r))

    others = pl.ds(1, groups - 1)
    twins = pl.ds(groups + 1, groups - 1)
    all_asks = all_of(0, want_ref.at[others], ask_ref.at[others])
    all_near = all_of(1, out_ref.at[pl.ds(1, near - 1)], near_ref.at[pl.ds(1, near - 1)])
    all_far = all_of(2, out_ref.at[pl.ds(near, groups - near)], far_ref)
    all_twin = all_of(3, out_ref.at[twins], twin_ref.at[others])
    all_first = all_of(4, back_ref.at[others], home_ref.at[others])
    all_last = all_of(5, back_ref.at[twins], home_ref.at[twins])
    rest_x = pl.ds(0, rows_x - 1)
    all_across = all_of(6, across_ref.at[rest_x], across_ref.at[rest_x])
    all_along = all_of(7, along_ref.at[others], along_ref.at[others])

    def each(first, last, body):
        def step(r, carry):
            body(r)
            return carry

        lax.fori_loop(first, last, step, 0)

    barrier = pltpu.get_barrier_semaphore()

    def greet(r):
        pl.semaphore_signal(barrier, inc=1, device_id=ahead(r), device_id_type=pl.DeviceIdType.MESH)

    def greet_across(r):
        pl.semaphore_signal(
            barrier, inc=1, device_id={"gx": lax.rem(my_row + r, rows_x)}, device_id_type=pl.DeviceIdType.MESH
        )

    each(1, groups, greet)
    each(1, rows_x, greet_across)
    for block in range(owned):
        block_ref[block] = features_ref[:, block * BLOCK : (block + 1) * BLOCK]
    pl.semaphore_wait(barrier, groups - 1 + rows_x - 1)

    each(1, groups, lambda r: ask(r).start())
    ask_ref[0] = want_ref[0]
    all_asks.wait_recv()
    fetch_plan = pltpu.make_async_copy(ask_ref, asked_ref, local_sem)
    fetch_plan.start()
    fetch_plan.wait()

    def load_out(place, r):
        out_ref[place * groups + r] = block_ref[jnp.maximum(asked_ref[r, 0, place], 0)]

    def send_near(r):
        load_out(0, r)
        fetch_near(r).start()

    def send_far(r):
        load_out(0, r)
        fetch_far(r).start()

    def send_twin(r):
        load_out(1, r)
        fetch_twin(r).start()

    each(1, near, send_near)
    each(near, groups, send_far)
    each(1, groups, send_twin)
    near_ref[0] = block_ref[jnp.maximum(asked_ref[0, 0, 0], 0)]
    twin_ref[0] = block_ref[jnp.maximum(asked_ref[0, 0, 1], 0)]

    def prepare(block):
        rows = read_rows(block_ref[block])
        left, _ = exponent_rows(rows)
        left_ref[block] = left_splits(left).T.astype(BF16)
        moment_ref[block] = moment_rows(rows)

    each(0, owned, prepare)
    result_ref[groups] = jnp.zeros_like(result_ref[groups])
    all_near.wait_recv()

    def visit(step, energy):
        @pl.when(step == head)
        def _():
            all_far.wait_recv()

        @pl.when(step == groups // 2)
        def _():
            all_twin.wait_recv()

        block = plan_ref[step]
        key = plan_ref[groups + step]
        factor = plan_ref[6 * groups + step].astype(F32)
        now_ref[...] = near_ref[jnp.minimum(key, near - 1)]

        @pl.when(step >= head)
        def _():
            far_block = far_ref[jnp.clip(key - near, 0, groups - near - 1)]
            now_ref[...] = jnp.where(key >= near, far_block, now_ref[...])

        @pl.when(step >= groups // 2)
        def _():
            twin_block = twin_ref[jnp.maximum(key - groups, 0)]
            now_ref[...] = jnp.where(key >= groups, twin_block, now_ref[...])

        rows = read_rows(now_ref[...])
        _, right = exponent_rows(rows)
        right = right_splits(right)
        second = moment_rows(rows)
        first = moment_ref[block]
        left = left_ref[block]

        def gaussians(tile):
            columns = slice(tile * TILE, (tile + 1) * TILE)
            value = jnp.exp2(dot(left, right[:, columns], 1, 0))
            high = value.astype(BF16)
            return high, (value - high.astype(F32)).astype(BF16)

        by_first = None
        by_second = []

        def contract(tile, high, low, by_first):
            columns = slice(tile * TILE, (tile + 1) * TILE)
            both = dot(second[:, columns], high, 1, 1)
            part = both[0:32] + both[32:64] + dot(second[0:32, columns], low, 1, 1)
            by_first = part if by_first is None else by_first + part
            both = dot(first, high, 1, 0)
            by_second.append(both[0:32] + both[32:64] + dot(first[0:32], low, 1, 0))
            return by_first

        tiles = BLOCK // TILE
        held = gaussians(0)
        for tile in range(tiles):
            later = gaussians(tile + 1) if tile + 1 < tiles else None
            by_first = contract(tile, *held, by_first)
            held = later
        mine_ref[step] = by_first
        out, share = finish(rows, jnp.concatenate(by_second, axis=1), factor)
        result_ref[step] = out[0:6]
        back_ref[step] = result_ref[plan_ref[2 * groups + step]]

        @pl.when(step >= 1)
        def _():
            give_back(0, step).start()

        return energy + share

    energy = lax.fori_loop(0, groups, visit, jnp.zeros((1, BLOCK), F32))
    share_ref[0] = jnp.full(share_ref.shape[1:], jnp.sum(energy) * (1.0 / BLOCK), F32)
    each(1, rows_x, lambda r: share_across(r).start())

    def send_last(r):
        back_ref[groups + r] = result_ref[plan_ref[3 * groups + r]]
        give_back(1, r).start()

    each(1, groups, send_last)
    back_ref[groups] = result_ref[plan_ref[3 * groups]]
    home_ref[0] = back_ref[0]
    home_ref[groups] = back_ref[groups]

    def close(block):
        def add(step, moments):
            weight = jnp.where(plan_ref[step] == block, plan_ref[6 * groups + step], 0).astype(F32)
            return moments + weight * mine_ref[step]

        moments = lax.fori_loop(0, groups, add, jnp.zeros((32, BLOCK), F32))
        out, _ = finish(read_rows(block_ref[block]), moments, 1.0)
        grad_ref[:, pl.ds(pl.multiple_of(block * BLOCK, BLOCK), BLOCK)] = out[0:6]

    each(0, 1, close)
    across_ref[my_row] = share_ref[0]
    all_across.wait_recv()
    total = across_ref[0]
    for r in range(1, rows_x):
        total = total + across_ref[r]
    share_ref[1] = total
    each(1, groups, lambda r: share_along(r).start())
    along_ref[me] = total
    each(1, owned, close)

    def gather(first, last):
        for start in range(0, BLOCK, TILE):

            def add(slot, sums, start=start):
                piece = home_ref[slot, :, start : start + TILE]
                wish = asked_ref[lax.rem(slot, groups), 0, slot // groups]
                return tuple(kept + jnp.where(wish == block, piece, 0.0) for block, kept in enumerate(sums))

            sums = lax.fori_loop(first, last, add, (jnp.zeros((6, TILE), F32),) * owned)
            for block in range(owned):
                grad_ref[:, block * BLOCK + start : block * BLOCK + start + TILE] += sums[block]

    all_first.wait_recv()
    gather(0, groups)
    all_along.wait_recv()
    total = lax.fori_loop(1, groups, lambda r, kept: kept + along_ref[r], along_ref[0])
    energy_ref[0, 0] = jnp.max(total)
    all_last.wait_recv()
    gather(groups, 2 * groups)
    for copies in (all_asks, all_near, all_far, all_twin, all_first, all_last, all_across, all_along):
        copies.wait_send()


def shards(features, first_slot, second_owner, second_slot, pair_count):
    owned = features.shape[1] // BLOCK
    entries = first_slot.shape[0]
    groups = lax.axis_size("gy")
    slots = 2 * groups
    near = groups // 2 + groups // 8
    me = lax.axis_index("gy")
    owners = second_owner[:, 0]
    order = jnp.arange(entries, dtype=jnp.int32)
    far = jnp.arange(slots, dtype=jnp.int32)
    live = order < pair_count[0]
    factors = jnp.where((owners == me) & (second_slot == first_slot), 1, 2)
    factors = jnp.where(live, factors, 0)
    rank = jnp.sum((owners[:, None] == owners[None, :]) & (order[None, :] < order[:, None]), axis=1)
    ahead = lax.rem(owners - me + groups, groups)
    distance = jnp.where(ahead <= groups // 2, jnp.maximum(2 * ahead - 1, 0), 2 * (groups - ahead))
    key = rank.astype(jnp.int32) * groups + distance
    place = jnp.sum(key[None, :] < key[:, None], axis=1).astype(jnp.int32)
    at_step = place[None, :] == order[:, None]
    at_slot = key[None, :] == far[:, None]

    def pick(table, values):
        return jnp.sum(jnp.where(table, values[None, :], 0), axis=1)

    want = pick(at_slot, second_slot + 1) - 1
    serve = pick(at_slot, place - groups) + groups
    plan = jnp.concatenate(
        [pick(at_step, first_slot), pick(at_step, key), serve, want, pick(at_step, factors)]
    ).astype(jnp.int32)
    lane = jnp.arange(128, dtype=jnp.int32)[None, :]
    asked = jnp.where(lane == 0, want[:groups, None], jnp.where(lane == 1, want[groups:, None], 0))

    smem = pl.BlockSpec(memory_space=pltpu.SMEM)
    vmem = pl.BlockSpec(memory_space=pltpu.VMEM)
    gradient, energy = pl.pallas_call(
        pair_kernel,
        out_shape=[
            jax.ShapeDtypeStruct((6, owned * BLOCK), F32),
            jax.ShapeDtypeStruct((1, 1), F32),
        ],
        in_specs=[smem, vmem, vmem],
        out_specs=[vmem, smem],
        scratch_shapes=[
            pltpu.VMEM((owned, 7, BLOCK), F32),
            pltpu.VMEM((owned, BLOCK, 48), BF16),
            pltpu.VMEM((owned, 64, BLOCK), BF16),
            pltpu.VMEM((groups, 1, 128), jnp.int32),
            pltpu.SMEM((groups, 1, 128), jnp.int32),
            pltpu.VMEM((slots, 7, BLOCK), F32),
            pltpu.VMEM((near, 7, BLOCK), F32),
            pltpu.VMEM((groups - near, 7, BLOCK), F32),
            pltpu.VMEM((groups, 7, BLOCK), F32),
            pltpu.VMEM((7, BLOCK), F32),
            pltpu.VMEM((groups, 32, BLOCK), F32),
            pltpu.VMEM((groups + 1, 6, BLOCK), F32),
            pltpu.VMEM((slots, 6, BLOCK), F32),
            pltpu.VMEM((slots, 6, BLOCK), F32),
            pltpu.VMEM((2, 8, 128), F32),
            pltpu.VMEM((lax.axis_size("gx"), 8, 128), F32),
            pltpu.VMEM((groups, 8, 128), F32),
            pltpu.SemaphoreType.DMA((8,)),
            pltpu.SemaphoreType.DMA((8,)),
            pltpu.SemaphoreType.DMA,
        ],
        compiler_params=pltpu.CompilerParams(
            vmem_limit_bytes=56 * 2**20, collective_id=0, has_side_effects=True
        ),
    )(plan, asked.reshape(groups, 1, 128), features)
    return (gradient, energy.reshape(()))


def solution(mesh):
    return jax.shard_map(
        shards,
        mesh=mesh,
        in_specs=(
            P(None, ("gx", "gy")),
            P(("gx", "gy")),
            P(("gx", "gy"), None),
            P(("gx", "gy")),
            P(("gx", "gy")),
        ),
        out_specs=(P(None, ("gx", "gy")), P()),
        check_vma=False,
    )
```

```python
import jax
import jax.numpy as jnp
from jax import lax
from jax.experimental import pallas as pl
from jax.experimental.pallas import tpu as pltpu
from jax.sharding import PartitionSpec as P

BLOCK = 1024
TILE = 256
DEPTH = 3
LOG2E = 1.4426950408889634
F32 = jnp.float32
BF16 = jnp.bfloat16


def dot(left, right, left_dim, right_dim):
    return lax.dot_general(
        left, right, (((left_dim,), (right_dim,)), ((), ())), preferred_element_type=F32
    )


def split_three(value):
    high = value.astype(BF16).astype(F32)
    rest = value - high
    mid = rest.astype(BF16).astype(F32)
    return high, mid, rest - mid


def select_rows(rows):
    index = lax.broadcasted_iota(jnp.int32, (8, BLOCK), 0)
    tile = jnp.zeros((8, BLOCK), F32)
    for place, row in enumerate(rows):
        tile = jnp.where(index == place, row, tile)
    return tile


def read_rows(block):
    return [block[row : row + 1] for row in range(7)]


def exponent_rows(rows):
    x, y, z = rows[:3]
    norm = (-0.5 * LOG2E) * (x * x + y * y + z * z)
    one = jnp.ones_like(x)
    left = select_rows([LOG2E * x, LOG2E * y, LOG2E * z, one, norm])
    right = select_rows([x, y, z, norm, one])
    return left, right


def left_splits(left):
    high, mid, low = split_three(left)
    return jnp.concatenate([high, high, mid, mid, high, low], axis=0)


def right_splits(right):
    high, mid, low = split_three(right)
    return jnp.concatenate([high, mid, high, mid, low, high], axis=0).astype(BF16)


def normal_products(rows):
    nx, ny, nz = rows[3:6]
    return select_rows([nx, ny, nz, nx, nx, ny]) * select_rows([nx, ny, nz, ny, nz, nz])


def moment_rows(rows):
    x, y, z, w = rows[0], rows[1], rows[2], rows[6]
    base = normal_products(rows) * w
    full = jnp.concatenate([base, base * x, base * y, base * z], axis=0)
    high = full.astype(BF16)
    low = (full - high.astype(F32)).astype(BF16)
    return jnp.concatenate([high, low], axis=0)


def finish(rows, moments, factor):
    x, y, z, nx, ny, nz, w = rows
    index = lax.broadcasted_iota(jnp.int32, (8, BLOCK), 0)
    doubled = normal_products(rows) * jnp.where(index < 3, 1.0, 2.0)
    mass = w * factor
    m0 = moments[0:8]
    sums = [
        jnp.sum(doubled * moments[8 * part : 8 * part + 8], axis=0, keepdims=True) * mass
        for part in range(4)
    ]
    xx, yy, zz, xy, xz, yz = [m0[row : row + 1] for row in range(6)]
    twice = 2.0 * mass
    out = select_rows(
        [
            sums[1] - x * sums[0],
            sums[2] - y * sums[0],
            sums[3] - z * sums[0],
            twice * (nx * xx + ny * xy + nz * xz),
            twice * (nx * xy + ny * yy + nz * yz),
            twice * (nx * xz + ny * yz + nz * zz),
        ]
    )
    return out, sums[0]


def pair_kernel(
    plan_ref, want_ref, features_ref,
    grad_ref, energy_ref,
    block_ref, left_ref, moment_ref, ask_ref, asked_ref, out_ref,
    near_ref, far_ref, twin_ref, now_ref, mine_ref, result_ref, back_ref, home_ref,
    share_ref, across_ref, along_ref, past_ref, high_ref, low_ref, column_ref, partial_ref,
    send_sem, recv_sem, local_sem,
):
    groups = want_ref.shape[0]
    rows_x = lax.axis_size("gx")
    owned = block_ref.shape[0]
    near = near_ref.shape[0]
    head = near - groups // 2
    me = lax.axis_index("gy")
    my_row = lax.axis_index("gx")

    def offset(r):
        half, odd = (r + 1) // 2, lax.rem(r, 2)
        return odd * half + (1 - odd) * (groups - half)

    def ahead(r):
        return {"gy": lax.rem(me + offset(r), groups)}

    def behind(r):
        return {"gy": lax.rem(me + 2 * groups - offset(r), groups)}

    def remote(kind, source, target, device):
        return pltpu.make_async_remote_copy(
            src_ref=source, dst_ref=target, send_sem=send_sem.at[kind], recv_sem=recv_sem.at[kind],
            device_id=device, device_id_type=pl.DeviceIdType.MESH,
        )

    def all_of(kind, source, target):
        return remote(kind, source, target, ahead(1))

    def ask(r):
        return remote(0, want_ref.at[r], ask_ref.at[r], ahead(r))

    def fetch_near(r):
        return remote(1, out_ref.at[r], near_ref.at[r], behind(r))

    def fetch_far(r):
        return remote(2, out_ref.at[r], far_ref.at[r - near], behind(r))

    def fetch_twin(r):
        return remote(3, out_ref.at[groups + r], twin_ref.at[r], behind(r))

    def give_back(rank, r):
        return remote(4 + rank, back_ref.at[rank * groups + r], home_ref.at[rank * groups + r], ahead(r))

    def share_across(r):
        return remote(6, share_ref.at[0], across_ref.at[my_row], {"gx": lax.rem(my_row + r, rows_x)})

    def share_along(r):
        return remote(7, share_ref.at[1], along_ref.at[me], ahead(r))

    others = pl.ds(1, groups - 1)
    twins = pl.ds(groups + 1, groups - 1)
    all_asks = all_of(0, want_ref.at[others], ask_ref.at[others])
    all_near = all_of(1, out_ref.at[pl.ds(1, near - 1)], near_ref.at[pl.ds(1, near - 1)])
    all_far = all_of(2, out_ref.at[pl.ds(near, groups - near)], far_ref)
    all_twin = all_of(3, out_ref.at[twins], twin_ref.at[others])
    all_first = all_of(4, back_ref.at[others], home_ref.at[others])
    all_last = all_of(5, back_ref.at[twins], home_ref.at[twins])
    rest_x = pl.ds(0, rows_x - 1)
    all_across = all_of(6, across_ref.at[rest_x], across_ref.at[rest_x])
    all_along = all_of(7, along_ref.at[others], along_ref.at[others])

    def each(first, last, body):
        def step(r, carry):
            body(r)
            return carry

        lax.fori_loop(first, last, step, 0)

    barrier = pltpu.get_barrier_semaphore()

    def greet(r):
        pl.semaphore_signal(barrier, inc=1, device_id=ahead(r), device_id_type=pl.DeviceIdType.MESH)

    def greet_across(r):
        pl.semaphore_signal(
            barrier, inc=1, device_id={"gx": lax.rem(my_row + r, rows_x)}, device_id_type=pl.DeviceIdType.MESH
        )

    each(1, groups, greet)
    each(1, rows_x, greet_across)
    for block in range(owned):
        block_ref[block] = features_ref[:, block * BLOCK : (block + 1) * BLOCK]
    pl.semaphore_wait(barrier, groups - 1 + rows_x - 1)

    each(1, groups, lambda r: ask(r).start())
    ask_ref[0] = want_ref[0]
    all_asks.wait_recv()
    fetch_plan = pltpu.make_async_copy(ask_ref, asked_ref, local_sem)
    fetch_plan.start()
    fetch_plan.wait()

    def load_out(place, r):
        out_ref[place * groups + r] = block_ref[jnp.maximum(asked_ref[r, 0, place], 0)]

    def send_near(r):
        load_out(0, r)
        fetch_near(r).start()

    def send_far(r):
        load_out(0, r)
        fetch_far(r).start()

    def send_twin(r):
        load_out(1, r)
        fetch_twin(r).start()

    each(1, near, send_near)
    each(near, groups, send_far)
    each(1, groups, send_twin)
    near_ref[0] = block_ref[jnp.maximum(asked_ref[0, 0, 0], 0)]
    twin_ref[0] = block_ref[jnp.maximum(asked_ref[0, 0, 1], 0)]

    def prepare(block):
        rows = read_rows(block_ref[block])
        left, _ = exponent_rows(rows)
        left_ref[block] = left_splits(left).T.astype(BF16)
        moment_ref[block] = moment_rows(rows)

    each(0, owned, prepare)
    result_ref[groups] = jnp.zeros_like(result_ref[groups])
    all_near.wait_recv()

    tiles = BLOCK // TILE
    chunks = tiles * tiles

    def cut(index):
        return slice(index * TILE, (index + 1) * TILE)

    def first_terms(second, high, low):
        both = dot(second, high, 1, 1)
        return both[0:32] + both[32:64] + dot(second[0:32], low, 1, 1)

    def second_terms(first, high, low):
        both = dot(first, high, 1, 0)
        return both[0:32] + both[32:64] + dot(first[0:32], low, 1, 0)

    def settle(entry, number, last_column):
        place = number + DEPTH
        high, low = high_ref[cut(place)], low_ref[cut(place)]
        rows = cut(tiles + number)
        mine_ref[entry, :, rows] += first_terms(column_ref[...], high, low)
        first = moment_ref[plan_ref[entry], :, rows]
        return last_column + second_terms(first, high, low)

    def conclude(entry, last_column):
        moments = jnp.concatenate([partial_ref[:, : BLOCK - TILE], last_column], axis=1)
        factor = plan_ref[6 * groups + entry].astype(F32)
        out, share = finish(read_rows(past_ref[...]), moments, factor)
        result_ref[entry] = out[0:6]
        return share

    def visit(step, energy):
        past_ref[...] = now_ref[...]

        @pl.when(step == head)
        def _():
            all_far.wait_recv()

        @pl.when(step == groups // 2)
        def _():
            all_twin.wait_recv()

        block = plan_ref[step]
        key = plan_ref[groups + step]
        now_ref[...] = near_ref[jnp.minimum(key, near - 1)]

        @pl.when(step >= head)
        def _():
            far_block = far_ref[jnp.clip(key - near, 0, groups - near - 1)]
            now_ref[...] = jnp.where(key >= near, far_block, now_ref[...])

        @pl.when(step >= groups // 2)
        def _():
            twin_block = twin_ref[jnp.maximum(key - groups, 0)]
            now_ref[...] = jnp.where(key >= groups, twin_block, now_ref[...])

        before = jnp.maximum(step - 1, 0)
        rows = read_rows(now_ref[...])
        _, right = exponent_rows(rows)
        right = right_splits(right)
        second = moment_rows(rows)
        first = moment_ref[block]
        left = left_ref[block]
        last_column = partial_ref[:, BLOCK - TILE :]
        by_first = [None] * tiles
        by_second = [None] * tiles
        flying = {}

        def add(sums, index, term):
            sums[index] = term if sums[index] is None else sums[index] + term

        for chunk in range(chunks):
            column, row = divmod(chunk, tiles)
            value = jnp.exp2(dot(left[cut(row)], right[:, cut(column)], 1, 0))
            high = value.astype(BF16)
            flying[chunk] = high, (value - high.astype(F32)).astype(BF16)
            if chunk < DEPTH:
                last_column = settle(before, chunk - DEPTH, last_column)
            if chunk == DEPTH - 1:
                energy = energy + conclude(before, last_column)
            if chunk >= DEPTH:
                column, row = divmod(chunk - DEPTH, tiles)
                high, low = flying.pop(chunk - DEPTH)
                add(by_first, row, first_terms(second[:, cut(column)], high, low))
                add(by_second, column, second_terms(first[:, cut(row)], high, low))
        for place in range(DEPTH):
            high_ref[cut(place)], low_ref[cut(place)] = flying[chunks - DEPTH + place]
        column_ref[...] = second[:, BLOCK - TILE :]
        partial_ref[...] = jnp.concatenate(by_second, axis=1)
        mine_ref[step] = jnp.concatenate(by_first, axis=1)
        back_ref[before] = result_ref[plan_ref[2 * groups + before]]

        @pl.when(step >= 2)
        def _():
            give_back(0, step - 1).start()

        return energy

    for held in (now_ref, high_ref, low_ref, column_ref, partial_ref):
        held[...] = jnp.zeros_like(held)
    mine_ref[0] = jnp.zeros_like(mine_ref[0])
    energy = lax.fori_loop(0, groups, visit, jnp.zeros((1, BLOCK), F32))
    past_ref[...] = now_ref[...]
    last_column = partial_ref[:, BLOCK - TILE :]
    for number in range(-DEPTH, 0):
        last_column = settle(groups - 1, number, last_column)
    energy = energy + conclude(groups - 1, last_column)
    back_ref[groups - 1] = result_ref[plan_ref[3 * groups - 1]]
    give_back(0, groups - 1).start()
    share_ref[0] = jnp.full(share_ref.shape[1:], jnp.sum(energy) * (1.0 / BLOCK), F32)
    each(1, rows_x, lambda r: share_across(r).start())

    def send_last(r):
        back_ref[groups + r] = result_ref[plan_ref[3 * groups + r]]
        give_back(1, r).start()

    each(1, groups, send_last)
    back_ref[groups] = result_ref[plan_ref[3 * groups]]
    home_ref[0] = back_ref[0]
    home_ref[groups] = back_ref[groups]

    def close(block):
        def add(step, moments):
            weight = jnp.where(plan_ref[step] == block, plan_ref[6 * groups + step], 0).astype(F32)
            return moments + weight * mine_ref[step]

        moments = lax.fori_loop(0, groups, add, jnp.zeros((32, BLOCK), F32))
        out, _ = finish(read_rows(block_ref[block]), moments, 1.0)
        grad_ref[:, pl.ds(pl.multiple_of(block * BLOCK, BLOCK), BLOCK)] = out[0:6]

    each(0, 1, close)
    across_ref[my_row] = share_ref[0]
    all_across.wait_recv()
    total = across_ref[0]
    for r in range(1, rows_x):
        total = total + across_ref[r]
    share_ref[1] = total
    each(1, groups, lambda r: share_along(r).start())
    along_ref[me] = total
    each(1, owned, close)

    def gather(first, last):
        for start in range(0, BLOCK, TILE):

            def add(slot, sums, start=start):
                piece = home_ref[slot, :, start : start + TILE]
                wish = asked_ref[lax.rem(slot, groups), 0, slot // groups]
                return tuple(kept + jnp.where(wish == block, piece, 0.0) for block, kept in enumerate(sums))

            sums = lax.fori_loop(first, last, add, (jnp.zeros((6, TILE), F32),) * owned)
            for block in range(owned):
                grad_ref[:, block * BLOCK + start : block * BLOCK + start + TILE] += sums[block]

    all_first.wait_recv()
    gather(0, groups)
    all_along.wait_recv()
    total = lax.fori_loop(1, groups, lambda r, kept: kept + along_ref[r], along_ref[0])
    energy_ref[0, 0] = jnp.max(total)
    all_last.wait_recv()
    gather(groups, 2 * groups)
    for copies in (all_asks, all_near, all_far, all_twin, all_first, all_last, all_across, all_along):
        copies.wait_send()


def shards(features, first_slot, second_owner, second_slot, pair_count):
    owned = features.shape[1] // BLOCK
    entries = first_slot.shape[0]
    groups = lax.axis_size("gy")
    slots = 2 * groups
    near = groups // 2 + max(1, groups // 16)
    me = lax.axis_index("gy")
    owners = second_owner[:, 0]
    order = jnp.arange(entries, dtype=jnp.int32)
    far = jnp.arange(slots, dtype=jnp.int32)
    live = order < pair_count[0]
    factors = jnp.where((owners == me) & (second_slot == first_slot), 1, 2)
    factors = jnp.where(live, factors, 0)
    rank = jnp.sum((owners[:, None] == owners[None, :]) & (order[None, :] < order[:, None]), axis=1)
    ahead = lax.rem(owners - me + groups, groups)
    distance = jnp.where(ahead <= groups // 2, jnp.maximum(2 * ahead - 1, 0), 2 * (groups - ahead))
    key = rank.astype(jnp.int32) * groups + distance
    place = jnp.sum(key[None, :] < key[:, None], axis=1).astype(jnp.int32)
    at_step = place[None, :] == order[:, None]
    at_slot = key[None, :] == far[:, None]

    def pick(table, values):
        return jnp.sum(jnp.where(table, values[None, :], 0), axis=1)

    want = pick(at_slot, second_slot + 1) - 1
    serve = pick(at_slot, place - groups) + groups
    plan = jnp.concatenate(
        [pick(at_step, first_slot), pick(at_step, key), serve, want, pick(at_step, factors)]
    ).astype(jnp.int32)
    lane = jnp.arange(128, dtype=jnp.int32)[None, :]
    asked = jnp.where(lane == 0, want[:groups, None], jnp.where(lane == 1, want[groups:, None], 0))

    smem = pl.BlockSpec(memory_space=pltpu.SMEM)
    vmem = pl.BlockSpec(memory_space=pltpu.VMEM)
    gradient, energy = pl.pallas_call(
        pair_kernel,
        out_shape=[
            jax.ShapeDtypeStruct((6, owned * BLOCK), F32),
            jax.ShapeDtypeStruct((1, 1), F32),
        ],
        in_specs=[smem, vmem, vmem],
        out_specs=[vmem, smem],
        scratch_shapes=[
            pltpu.VMEM((owned, 7, BLOCK), F32),
            pltpu.VMEM((owned, BLOCK, 48), BF16),
            pltpu.VMEM((owned, 64, BLOCK), BF16),
            pltpu.VMEM((groups, 1, 128), jnp.int32),
            pltpu.SMEM((groups, 1, 128), jnp.int32),
            pltpu.VMEM((slots, 7, BLOCK), F32),
            pltpu.VMEM((near, 7, BLOCK), F32),
            pltpu.VMEM((groups - near, 7, BLOCK), F32),
            pltpu.VMEM((groups, 7, BLOCK), F32),
            pltpu.VMEM((7, BLOCK), F32),
            pltpu.VMEM((groups, 32, BLOCK), F32),
            pltpu.VMEM((groups + 1, 6, BLOCK), F32),
            pltpu.VMEM((slots, 6, BLOCK), F32),
            pltpu.VMEM((slots, 6, BLOCK), F32),
            pltpu.VMEM((2, 8, 128), F32),
            pltpu.VMEM((lax.axis_size("gx"), 8, 128), F32),
            pltpu.VMEM((groups, 8, 128), F32),
            pltpu.VMEM((7, BLOCK), F32),
            pltpu.VMEM((DEPTH * TILE, TILE), BF16),
            pltpu.VMEM((DEPTH * TILE, TILE), BF16),
            pltpu.VMEM((64, TILE), BF16),
            pltpu.VMEM((32, BLOCK), F32),
            pltpu.SemaphoreType.DMA((8,)),
            pltpu.SemaphoreType.DMA((8,)),
            pltpu.SemaphoreType.DMA,
        ],
        compiler_params=pltpu.CompilerParams(
            vmem_limit_bytes=56 * 2**20, collective_id=0, has_side_effects=True
        ),
    )(plan, asked.reshape(groups, 1, 128), features)
    return (gradient, energy.reshape(()))


def solution(mesh):
    return jax.shard_map(
        shards,
        mesh=mesh,
        in_specs=(
            P(None, ("gx", "gy")),
            P(("gx", "gy")),
            P(("gx", "gy"), None),
            P(("gx", "gy")),
            P(("gx", "gy")),
        ),
        out_specs=(P(None, ("gx", "gy")), P()),
        check_vma=False,
    )
```

```python
import jax
import jax.numpy as jnp
from jax import lax
from jax.experimental import pallas as pl
from jax.experimental.pallas import tpu as pltpu
from jax.sharding import PartitionSpec as P

BLOCK = 1024
TILE = 256
DEPTH = 3
LOG2E = 1.4426950408889634
F32 = jnp.float32
BF16 = jnp.bfloat16


def dot(left, right, left_dim, right_dim):
    return lax.dot_general(
        left, right, (((left_dim,), (right_dim,)), ((), ())), preferred_element_type=F32
    )


def split_three(value):
    high = value.astype(BF16).astype(F32)
    rest = value - high
    mid = rest.astype(BF16).astype(F32)
    return high, mid, rest - mid


def select_rows(rows):
    index = lax.broadcasted_iota(jnp.int32, (8, BLOCK), 0)
    tile = jnp.zeros((8, BLOCK), F32)
    for place, row in enumerate(rows):
        tile = jnp.where(index == place, row, tile)
    return tile


def read_rows(block):
    return [block[row : row + 1] for row in range(7)]


def exponent_rows(rows):
    x, y, z = rows[:3]
    norm = (-0.5 * LOG2E) * (x * x + y * y + z * z)
    one = jnp.ones_like(x)
    left = select_rows([LOG2E * x, LOG2E * y, LOG2E * z, one, norm])
    right = select_rows([x, y, z, norm, one])
    return left, right


def left_splits(left):
    high, mid, low = split_three(left)
    return jnp.concatenate([high, high, mid, mid, high, low], axis=0)


def right_splits(right):
    high, mid, low = split_three(right)
    return jnp.concatenate([high, mid, high, mid, low, high], axis=0).astype(BF16)


def normal_products(rows):
    nx, ny, nz = rows[3:6]
    return select_rows([nx, ny, nz, nx, nx, ny]) * select_rows([nx, ny, nz, ny, nz, nz])


def moment_rows(rows):
    x, y, z, w = rows[0], rows[1], rows[2], rows[6]
    base = normal_products(rows) * w
    full = jnp.concatenate([base, base * x, base * y, base * z], axis=0)
    high = full.astype(BF16)
    low = (full - high.astype(F32)).astype(BF16)
    return jnp.concatenate([high, low], axis=0)


def finish(rows, moments, factor):
    x, y, z, nx, ny, nz, w = rows
    index = lax.broadcasted_iota(jnp.int32, (8, BLOCK), 0)
    doubled = normal_products(rows) * jnp.where(index < 3, 1.0, 2.0)
    mass = w * factor
    m0 = moments[0:8]
    sums = [
        jnp.sum(doubled * moments[8 * part : 8 * part + 8], axis=0, keepdims=True) * mass
        for part in range(4)
    ]
    xx, yy, zz, xy, xz, yz = [m0[row : row + 1] for row in range(6)]
    twice = 2.0 * mass
    out = select_rows(
        [
            sums[1] - x * sums[0],
            sums[2] - y * sums[0],
            sums[3] - z * sums[0],
            twice * (nx * xx + ny * xy + nz * xz),
            twice * (nx * xy + ny * yy + nz * yz),
            twice * (nx * xz + ny * yz + nz * zz),
        ]
    )
    return out, sums[0]


def pair_kernel(
    plan_ref, want_ref, features_ref,
    grad_ref, energy_ref,
    block_ref, left_ref, moment_ref, ask_ref, asked_ref, out_ref,
    near_ref, far_ref, twin_ref, now_ref, mine_ref, result_ref, back_ref, home_ref,
    share_ref, across_ref, along_ref, past_ref, high_ref, low_ref, column_ref, partial_ref, local_ref,
    send_sem, recv_sem, local_sem,
):
    groups = want_ref.shape[0]
    rows_x = lax.axis_size("gx")
    owned = block_ref.shape[0]
    near = near_ref.shape[0]
    head = near - groups // 2
    me = lax.axis_index("gy")
    my_row = lax.axis_index("gx")

    def offset(r):
        half, odd = (r + 1) // 2, lax.rem(r, 2)
        return odd * half + (1 - odd) * (groups - half)

    def ahead(r):
        return {"gy": lax.rem(me + offset(r), groups)}

    def behind(r):
        return {"gy": lax.rem(me + 2 * groups - offset(r), groups)}

    def remote(kind, source, target, device):
        return pltpu.make_async_remote_copy(
            src_ref=source, dst_ref=target, send_sem=send_sem.at[kind], recv_sem=recv_sem.at[kind],
            device_id=device, device_id_type=pl.DeviceIdType.MESH,
        )

    def all_of(kind, source, target):
        return remote(kind, source, target, ahead(1))

    def ask(r):
        return remote(0, want_ref.at[r], ask_ref.at[r], ahead(r))

    def fetch_near(r):
        return remote(1, out_ref.at[r], near_ref.at[r], behind(r))

    def fetch_far(r):
        return remote(2, out_ref.at[r], far_ref.at[r - near], behind(r))

    def fetch_twin(r):
        return remote(3, out_ref.at[groups + r], twin_ref.at[r], behind(r))

    def give_back(rank, r):
        return remote(4 + rank, back_ref.at[rank * groups + r], home_ref.at[rank * groups + r], ahead(r))

    def share_across(r):
        return remote(6, share_ref.at[0], across_ref.at[my_row], {"gx": lax.rem(my_row + r, rows_x)})

    def share_along(r):
        return remote(7, share_ref.at[1], along_ref.at[me], ahead(r))

    others = pl.ds(1, groups - 1)
    twins = pl.ds(groups + 1, groups - 1)
    all_asks = all_of(0, want_ref.at[others], ask_ref.at[others])
    all_near = all_of(1, out_ref.at[pl.ds(1, near - 1)], near_ref.at[pl.ds(1, near - 1)])
    all_far = all_of(2, out_ref.at[pl.ds(near, groups - near)], far_ref)
    all_twin = all_of(3, out_ref.at[twins], twin_ref.at[others])
    all_first = all_of(4, back_ref.at[others], home_ref.at[others])
    all_last = all_of(5, back_ref.at[twins], home_ref.at[twins])
    rest_x = pl.ds(0, rows_x - 1)
    all_across = all_of(6, across_ref.at[rest_x], across_ref.at[rest_x])
    all_along = all_of(7, along_ref.at[others], along_ref.at[others])

    def each(first, last, body):
        def step(r, carry):
            body(r)
            return carry

        lax.fori_loop(first, last, step, 0)

    barrier = pltpu.get_barrier_semaphore()

    def greet(r):
        pl.semaphore_signal(barrier, inc=1, device_id=ahead(r), device_id_type=pl.DeviceIdType.MESH)

    def greet_across(r):
        pl.semaphore_signal(
            barrier, inc=1, device_id={"gx": lax.rem(my_row + r, rows_x)}, device_id_type=pl.DeviceIdType.MESH
        )

    each(1, groups, greet)
    each(1, rows_x, greet_across)
    for block in range(owned):
        block_ref[block] = features_ref[:, block * BLOCK : (block + 1) * BLOCK]
    pl.semaphore_wait(barrier, groups - 1 + rows_x - 1)

    each(1, groups, lambda r: ask(r).start())
    ask_ref[0] = want_ref[0]
    all_asks.wait_recv()
    fetch_plan = pltpu.make_async_copy(ask_ref, asked_ref, local_sem)
    fetch_plan.start()
    fetch_plan.wait()

    def load_out(place, r):
        out_ref[place * groups + r] = block_ref[jnp.maximum(asked_ref[r, 0, place], 0)]

    def send_near(r):
        load_out(0, r)
        fetch_near(r).start()

    def send_far(r):
        load_out(0, r)
        fetch_far(r).start()

    def send_twin(r):
        load_out(1, r)
        fetch_twin(r).start()

    each(1, near, send_near)
    each(near, groups, send_far)
    each(1, groups, send_twin)
    near_ref[0] = block_ref[jnp.maximum(asked_ref[0, 0, 0], 0)]
    twin_ref[0] = block_ref[jnp.maximum(asked_ref[0, 0, 1], 0)]

    def prepare(block):
        rows = read_rows(block_ref[block])
        left, _ = exponent_rows(rows)
        left_ref[block] = left_splits(left).T.astype(BF16)
        moment_ref[block] = moment_rows(rows)

    each(0, owned, prepare)
    result_ref[groups] = jnp.zeros_like(result_ref[groups])
    all_near.wait_recv()

    tiles = BLOCK // TILE
    chunks = tiles * tiles

    def cut(index):
        return slice(index * TILE, (index + 1) * TILE)

    def first_terms(second, high, low):
        both = dot(second, high, 1, 1)
        return both[0:32] + both[32:64] + dot(second[0:32], low, 1, 1)

    def second_terms(first, high, low):
        both = dot(first, high, 1, 0)
        return both[0:32] + both[32:64] + dot(first[0:32], low, 1, 0)

    def settle(entry, number, last_column):
        place = number + DEPTH
        high, low = high_ref[cut(place)], low_ref[cut(place)]
        rows = cut(tiles + number)
        mine_ref[:, rows] += first_terms(column_ref[...], high, low)
        first = moment_ref[plan_ref[entry], :, rows]
        return last_column + second_terms(first, high, low)

    def conclude(entry, last_column):
        moments = jnp.concatenate([partial_ref[:, : BLOCK - TILE], last_column], axis=1)
        factor = plan_ref[6 * groups + entry].astype(F32)
        out, share = finish(read_rows(past_ref[...]), moments, factor)
        result_ref[entry] = out[0:6]
        block = plan_ref[entry]
        out, _ = finish(read_rows(block_ref[block]), mine_ref[...], factor)
        for own in range(owned):
            local_ref[own] += jnp.where(block == own, out, 0.0)
        return share

    def visit(step, energy):
        past_ref[...] = now_ref[...]

        @pl.when(step == head)
        def _():
            all_far.wait_recv()

        @pl.when(step == groups // 2)
        def _():
            all_twin.wait_recv()

        block = plan_ref[step]
        key = plan_ref[groups + step]
        now_ref[...] = near_ref[jnp.minimum(key, near - 1)]

        @pl.when(step >= head)
        def _():
            far_block = far_ref[jnp.clip(key - near, 0, groups - near - 1)]
            now_ref[...] = jnp.where(key >= near, far_block, now_ref[...])

        @pl.when(step >= groups // 2)
        def _():
            twin_block = twin_ref[jnp.maximum(key - groups, 0)]
            now_ref[...] = jnp.where(key >= groups, twin_block, now_ref[...])

        before = jnp.maximum(step - 1, 0)
        rows = read_rows(now_ref[...])
        _, right = exponent_rows(rows)
        right = right_splits(right)
        second = moment_rows(rows)
        first = moment_ref[block]
        left = left_ref[block]
        last_column = partial_ref[:, BLOCK - TILE :]
        by_first = [None] * tiles
        by_second = [None] * tiles
        flying = {}

        def add(sums, index, term):
            sums[index] = term if sums[index] is None else sums[index] + term

        for chunk in range(chunks):
            column, row = divmod(chunk, tiles)
            value = jnp.exp2(dot(left[cut(row)], right[:, cut(column)], 1, 0))
            high = value.astype(BF16)
            flying[chunk] = high, (value - high.astype(F32)).astype(BF16)
            if chunk < DEPTH:
                last_column = settle(before, chunk - DEPTH, last_column)
            if chunk == DEPTH - 1:
                energy = energy + conclude(before, last_column)
            if chunk >= DEPTH:
                column, row = divmod(chunk - DEPTH, tiles)
                high, low = flying.pop(chunk - DEPTH)
                add(by_first, row, first_terms(second[:, cut(column)], high, low))
                add(by_second, column, second_terms(first[:, cut(row)], high, low))
        for place in range(DEPTH):
            high_ref[cut(place)], low_ref[cut(place)] = flying[chunks - DEPTH + place]
        column_ref[...] = second[:, BLOCK - TILE :]
        partial_ref[...] = jnp.concatenate(by_second, axis=1)
        mine_ref[...] = jnp.concatenate(by_first, axis=1)
        back_ref[before] = result_ref[plan_ref[2 * groups + before]]

        @pl.when(step >= 2)
        def _():
            give_back(0, step - 1).start()

        return energy

    for held in (now_ref, high_ref, low_ref, column_ref, partial_ref, mine_ref, local_ref):
        held[...] = jnp.zeros_like(held)
    energy = lax.fori_loop(0, groups, visit, jnp.zeros((1, BLOCK), F32))
    past_ref[...] = now_ref[...]
    last_column = partial_ref[:, BLOCK - TILE :]
    for number in range(-DEPTH, 0):
        last_column = settle(groups - 1, number, last_column)
    energy = energy + conclude(groups - 1, last_column)
    back_ref[groups - 1] = result_ref[plan_ref[3 * groups - 1]]
    give_back(0, groups - 1).start()
    share_ref[0] = jnp.full(share_ref.shape[1:], jnp.sum(energy) * (1.0 / BLOCK), F32)
    each(1, rows_x, lambda r: share_across(r).start())

    def send_last(r):
        back_ref[groups + r] = result_ref[plan_ref[3 * groups + r]]
        give_back(1, r).start()

    each(1, groups // 2, send_last)
    all_across.wait_recv()
    across_ref[my_row] = share_ref[0]
    total = across_ref[0]
    for r in range(1, rows_x):
        total = total + across_ref[r]
    share_ref[1] = total
    each(1, groups, lambda r: share_along(r).start())
    along_ref[me] = total
    each(groups // 2, groups, send_last)
    back_ref[groups] = result_ref[plan_ref[3 * groups]]
    home_ref[0] = back_ref[0]
    home_ref[groups] = back_ref[groups]

    def gather(first, last, into):
        for start in range(0, BLOCK, TILE):

            def add(slot, sums, start=start):
                piece = home_ref[slot, :, start : start + TILE]
                wish = asked_ref[lax.rem(slot, groups), 0, slot // groups]
                return tuple(kept + jnp.where(wish == block, piece, 0.0) for block, kept in enumerate(sums))

            sums = lax.fori_loop(first, last, add, (jnp.zeros((6, TILE), F32),) * owned)
            for block in range(owned):
                columns = slice(block * BLOCK + start, block * BLOCK + start + TILE)
                grad_ref[:, columns] = into(block, start, columns) + sums[block]

    all_first.wait_recv()
    gather(0, groups, lambda block, start, columns: local_ref[block, 0:6, start : start + TILE])
    all_along.wait_recv()
    total = lax.fori_loop(1, groups, lambda r, kept: kept + along_ref[r], along_ref[0])
    energy_ref[0, 0] = jnp.max(total)
    all_last.wait_recv()
    gather(groups, 2 * groups, lambda block, start, columns: grad_ref[:, columns])
    for copies in (all_asks, all_near, all_far, all_twin, all_first, all_last, all_across, all_along):
        copies.wait_send()


def shards(features, first_slot, second_owner, second_slot, pair_count):
    owned = features.shape[1] // BLOCK
    entries = first_slot.shape[0]
    groups = lax.axis_size("gy")
    slots = 2 * groups
    near = groups // 2 + max(1, groups // 16)
    me = lax.axis_index("gy")
    owners = second_owner[:, 0]
    order = jnp.arange(entries, dtype=jnp.int32)
    far = jnp.arange(slots, dtype=jnp.int32)
    live = order < pair_count[0]
    factors = jnp.where((owners == me) & (second_slot == first_slot), 1, 2)
    factors = jnp.where(live, factors, 0)
    rank = jnp.sum((owners[:, None] == owners[None, :]) & (order[None, :] < order[:, None]), axis=1)
    ahead = lax.rem(owners - me + groups, groups)
    distance = jnp.where(ahead <= groups // 2, jnp.maximum(2 * ahead - 1, 0), 2 * (groups - ahead))
    key = rank.astype(jnp.int32) * groups + distance
    place = jnp.sum(key[None, :] < key[:, None], axis=1).astype(jnp.int32)
    at_step = place[None, :] == order[:, None]
    at_slot = key[None, :] == far[:, None]

    def pick(table, values):
        return jnp.sum(jnp.where(table, values[None, :], 0), axis=1)

    want = pick(at_slot, second_slot + 1) - 1
    serve = pick(at_slot, place - groups) + groups
    plan = jnp.concatenate(
        [pick(at_step, first_slot), pick(at_step, key), serve, want, pick(at_step, factors)]
    ).astype(jnp.int32)
    lane = jnp.arange(128, dtype=jnp.int32)[None, :]
    asked = jnp.where(lane == 0, want[:groups, None], jnp.where(lane == 1, want[groups:, None], 0))

    smem = pl.BlockSpec(memory_space=pltpu.SMEM)
    vmem = pl.BlockSpec(memory_space=pltpu.VMEM)
    gradient, energy = pl.pallas_call(
        pair_kernel,
        out_shape=[
            jax.ShapeDtypeStruct((6, owned * BLOCK), F32),
            jax.ShapeDtypeStruct((1, 1), F32),
        ],
        in_specs=[smem, vmem, vmem],
        out_specs=[vmem, smem],
        scratch_shapes=[
            pltpu.VMEM((owned, 7, BLOCK), F32),
            pltpu.VMEM((owned, BLOCK, 48), BF16),
            pltpu.VMEM((owned, 64, BLOCK), BF16),
            pltpu.VMEM((groups, 1, 128), jnp.int32),
            pltpu.SMEM((groups, 1, 128), jnp.int32),
            pltpu.VMEM((slots, 7, BLOCK), F32),
            pltpu.VMEM((near, 7, BLOCK), F32),
            pltpu.VMEM((groups - near, 7, BLOCK), F32),
            pltpu.VMEM((groups, 7, BLOCK), F32),
            pltpu.VMEM((7, BLOCK), F32),
            pltpu.VMEM((32, BLOCK), F32),
            pltpu.VMEM((groups + 1, 6, BLOCK), F32),
            pltpu.VMEM((slots, 6, BLOCK), F32),
            pltpu.VMEM((slots, 6, BLOCK), F32),
            pltpu.VMEM((2, 8, 128), F32),
            pltpu.VMEM((lax.axis_size("gx"), 8, 128), F32),
            pltpu.VMEM((groups, 8, 128), F32),
            pltpu.VMEM((7, BLOCK), F32),
            pltpu.VMEM((DEPTH * TILE, TILE), BF16),
            pltpu.VMEM((DEPTH * TILE, TILE), BF16),
            pltpu.VMEM((64, TILE), BF16),
            pltpu.VMEM((32, BLOCK), F32),
            pltpu.VMEM((owned, 8, BLOCK), F32),
            pltpu.SemaphoreType.DMA((8,)),
            pltpu.SemaphoreType.DMA((8,)),
            pltpu.SemaphoreType.DMA,
        ],
        compiler_params=pltpu.CompilerParams(
            vmem_limit_bytes=56 * 2**20, collective_id=0, has_side_effects=True
        ),
    )(plan, asked.reshape(groups, 1, 128), features)
    return (gradient, energy.reshape(()))


def solution(mesh):
    return jax.shard_map(
        shards,
        mesh=mesh,
        in_specs=(
            P(None, ("gx", "gy")),
            P(("gx", "gy")),
            P(("gx", "gy"), None),
            P(("gx", "gy")),
            P(("gx", "gy")),
        ),
        out_specs=(P(None, ("gx", "gy")), P()),
        check_vma=False,
    )
```

```python
import jax
import jax.numpy as jnp
from jax import lax
from jax.experimental import pallas as pl
from jax.experimental.pallas import tpu as pltpu
from jax.sharding import PartitionSpec as P

BLOCK = 1024
TILE = 256
DEPTH = 3
LOG2E = 1.4426950408889634
F32 = jnp.float32
BF16 = jnp.bfloat16


def dot(left, right, left_dim, right_dim):
    return lax.dot_general(
        left, right, (((left_dim,), (right_dim,)), ((), ())), preferred_element_type=F32
    )


def split_three(value):
    high = value.astype(BF16).astype(F32)
    rest = value - high
    mid = rest.astype(BF16).astype(F32)
    return high, mid, rest - mid


def select_rows(rows):
    index = lax.broadcasted_iota(jnp.int32, (8, BLOCK), 0)
    tile = jnp.zeros((8, BLOCK), F32)
    for place, row in enumerate(rows):
        tile = jnp.where(index == place, row, tile)
    return tile


def read_rows(block):
    return [block[row : row + 1] for row in range(7)]


def exponent_rows(rows):
    x, y, z = rows[:3]
    norm = (-0.5 * LOG2E) * (x * x + y * y + z * z)
    one = jnp.ones_like(x)
    left = select_rows([LOG2E * x, LOG2E * y, LOG2E * z, one, norm])
    right = select_rows([x, y, z, norm, one])
    return left, right


def left_splits(left):
    high, mid, low = split_three(left)
    return jnp.concatenate([high, high, mid, mid, high, low], axis=0)


def right_splits(right):
    high, mid, low = split_three(right)
    return jnp.concatenate([high, mid, high, mid, low, high], axis=0).astype(BF16)


def normal_products(rows):
    nx, ny, nz = rows[3:6]
    return select_rows([nx, ny, nz, nx, nx, ny]) * select_rows([nx, ny, nz, ny, nz, nz])


def moment_rows(rows):
    x, y, z, w = rows[0], rows[1], rows[2], rows[6]
    base = normal_products(rows) * w
    full = jnp.concatenate([base, base * x, base * y, base * z], axis=0)
    high = full.astype(BF16)
    low = (full - high.astype(F32)).astype(BF16)
    return jnp.concatenate([high, low], axis=0)


def finish(rows, moments, factor):
    x, y, z, nx, ny, nz, w = rows
    index = lax.broadcasted_iota(jnp.int32, (8, BLOCK), 0)
    doubled = normal_products(rows) * jnp.where(index < 3, 1.0, 2.0)
    mass = w * factor
    m0 = moments[0:8]
    sums = [
        jnp.sum(doubled * moments[8 * part : 8 * part + 8], axis=0, keepdims=True) * mass
        for part in range(4)
    ]
    xx, yy, zz, xy, xz, yz = [m0[row : row + 1] for row in range(6)]
    twice = 2.0 * mass
    out = select_rows(
        [
            sums[1] - x * sums[0],
            sums[2] - y * sums[0],
            sums[3] - z * sums[0],
            twice * (nx * xx + ny * xy + nz * xz),
            twice * (nx * xy + ny * yy + nz * yz),
            twice * (nx * xz + ny * yz + nz * zz),
        ]
    )
    return out, sums[0]


def pair_kernel(
    plan_ref, want_ref, features_ref,
    grad_ref, energy_ref,
    block_ref, left_ref, moment_ref, ask_ref, asked_ref, out_ref,
    near_ref, far_ref, twin_ref, now_ref, mine_ref, result_ref, back_ref, home_ref,
    share_ref, across_ref, along_ref, past_ref, high_ref, low_ref, column_ref, partial_ref, local_ref, sums_ref,
    send_sem, recv_sem, local_sem,
):
    groups = want_ref.shape[0]
    rows_x = lax.axis_size("gx")
    owned = block_ref.shape[0]
    near = near_ref.shape[0]
    head = near - groups // 2
    me = lax.axis_index("gy")
    my_row = lax.axis_index("gx")

    def offset(r):
        if groups != 32:
            half, odd = (r + 1) // 2, lax.rem(r, 2)
            return odd * half + (1 - odd) * (groups - half)
        core = lax.rem(r, 2)
        ring = lax.rem(r // 2 + 4, 9)
        close = 8 * (ring // 3) + 2 * lax.rem(ring, 3) - 10 + core
        rest = jnp.maximum(r - 18, 0)
        across_z = 14 + 2 * (rest // 2) + core
        across_x = 8 * (jnp.maximum(rest - 8, 0) // 2) - 4 + core
        beyond, last = r // 18, rest // 8
        return 32 + (1 - beyond) * close + beyond * ((1 - last) * across_z + last * across_x)

    def ahead(r):
        return {"gy": lax.rem(me + offset(r), groups)}

    def behind(r):
        return {"gy": lax.rem(me + 3 * groups - offset(r), groups)}

    def remote(kind, source, target, device):
        return pltpu.make_async_remote_copy(
            src_ref=source, dst_ref=target, send_sem=send_sem.at[kind], recv_sem=recv_sem.at[kind],
            device_id=device, device_id_type=pl.DeviceIdType.MESH,
        )

    def all_of(kind, source, target):
        return remote(kind, source, target, ahead(1))

    def ask(r):
        return remote(0, want_ref.at[r], ask_ref.at[r], ahead(r))

    def fetch_near(r):
        return remote(1, out_ref.at[r], near_ref.at[r], behind(r))

    def fetch_far(r):
        return remote(2, out_ref.at[r], far_ref.at[r - near], behind(r))

    def fetch_twin(r):
        return remote(3, out_ref.at[groups + r], twin_ref.at[r], behind(r))

    def give_back(rank, r):
        return remote(4 + rank, back_ref.at[rank * groups + r], home_ref.at[rank * groups + r], ahead(r))

    def share_across(r):
        return remote(6, share_ref.at[0], across_ref.at[my_row], {"gx": lax.rem(my_row + r, rows_x)})

    def share_along(r):
        return remote(7, share_ref.at[1], along_ref.at[me], ahead(r))

    others = pl.ds(1, groups - 1)
    twins = pl.ds(groups + 1, groups - 1)
    all_asks = all_of(0, want_ref.at[others], ask_ref.at[others])
    all_near = all_of(1, out_ref.at[pl.ds(1, near - 1)], near_ref.at[pl.ds(1, near - 1)])
    all_far = all_of(2, out_ref.at[pl.ds(near, groups - near)], far_ref)
    all_twin = all_of(3, out_ref.at[twins], twin_ref.at[others])
    all_first = all_of(4, back_ref.at[others], home_ref.at[others])
    all_last = all_of(5, back_ref.at[twins], home_ref.at[twins])
    rest_x = pl.ds(0, rows_x - 1)
    all_across = all_of(6, across_ref.at[rest_x], across_ref.at[rest_x])
    all_along = all_of(7, along_ref.at[others], along_ref.at[others])

    def each(first, last, body):
        def step(r, carry):
            body(r)
            return carry

        lax.fori_loop(first, last, step, 0)

    barrier = pltpu.get_barrier_semaphore()

    def greet(r):
        pl.semaphore_signal(barrier, inc=1, device_id=ahead(r), device_id_type=pl.DeviceIdType.MESH)

    def greet_across(r):
        pl.semaphore_signal(
            barrier, inc=1, device_id={"gx": lax.rem(my_row + r, rows_x)}, device_id_type=pl.DeviceIdType.MESH
        )

    each(1, groups, greet)
    each(1, rows_x, greet_across)
    for block in range(owned):
        block_ref[block] = features_ref[:, block * BLOCK : (block + 1) * BLOCK]
    pl.semaphore_wait(barrier, groups - 1 + rows_x - 1)

    each(1, groups, lambda r: ask(r).start())
    ask_ref[0] = want_ref[0]
    all_asks.wait_recv()
    fetch_plan = pltpu.make_async_copy(ask_ref, asked_ref, local_sem)
    fetch_plan.start()
    fetch_plan.wait()

    def load_out(place, r):
        out_ref[place * groups + r] = block_ref[jnp.maximum(asked_ref[r, 0, place], 0)]

    def send_near(r):
        load_out(0, r)
        fetch_near(r).start()

    def send_far(r):
        load_out(0, r)
        fetch_far(r).start()

    def send_twin(r):
        load_out(1, r)
        fetch_twin(r).start()

    each(1, near, send_near)
    each(near, groups, send_far)
    each(1, groups, send_twin)
    near_ref[0] = block_ref[jnp.maximum(asked_ref[0, 0, 0], 0)]
    twin_ref[0] = block_ref[jnp.maximum(asked_ref[0, 0, 1], 0)]

    def prepare(block):
        rows = read_rows(block_ref[block])
        left, _ = exponent_rows(rows)
        left_ref[block] = left_splits(left).T.astype(BF16)
        moment_ref[block] = moment_rows(rows)

    each(0, owned, prepare)
    result_ref[groups] = jnp.zeros_like(result_ref[groups])
    all_near.wait_recv()

    tiles = BLOCK // TILE
    width, piece = BLOCK - BLOCK // 4, BLOCK // 8
    chunks = tiles * tiles

    def cut(index):
        return slice(index * TILE, (index + 1) * TILE)

    def first_terms(second, high, low):
        both = dot(second, high, 1, 1)
        return both[0:32] + both[32:64] + dot(second[0:32], low, 1, 1)

    def second_terms(first, high, low):
        both = dot(first, high, 1, 0)
        return both[0:32] + both[32:64] + dot(first[0:32], low, 1, 0)

    def settle(entry, number, last_column):
        place = number + DEPTH
        high, low = high_ref[cut(place)], low_ref[cut(place)]
        rows = cut(tiles + number)
        mine_ref[:, rows] += first_terms(column_ref[...], high, low)
        first = moment_ref[plan_ref[entry], :, rows]
        return last_column + second_terms(first, high, low)

    def pack(entry, out):
        result_ref[entry, 0:6] = out[0:6, :width]
        for part in range(6):
            top, start = 2 * (part % 3), width + (part // 3) * piece
            result_ref[entry, 6:8, part * piece : (part + 1) * piece] = out[top : top + 2, start : start + piece]

    def unpack(block):
        start = block * BLOCK
        local_ref[block, 0:6, :width] += sums_ref[block, 0:6]
        for part in range(6):
            top, place = 2 * (part % 3), width + (part // 3) * piece
            local_ref[block, top : top + 2, place : place + piece] += sums_ref[
                block, 6:8, part * piece : (part + 1) * piece
            ]
        grad_ref[:, start : start + BLOCK] = local_ref[block, 0:6]

    def conclude(entry, last_column):
        moments = jnp.concatenate([partial_ref[:, : BLOCK - TILE], last_column], axis=1)
        factor = plan_ref[6 * groups + entry].astype(F32)
        out, share = finish(read_rows(past_ref[...]), moments, factor)
        pack(entry, out)
        block = plan_ref[entry]
        out, _ = finish(read_rows(block_ref[block]), mine_ref[...], factor)
        for own in range(owned):
            local_ref[own] += jnp.where(block == own, out, 0.0)
        return share

    def visit(step, energy):
        past_ref[...] = now_ref[...]

        @pl.when(step == head)
        def _():
            all_far.wait_recv()

        @pl.when(step == groups // 2)
        def _():
            all_twin.wait_recv()

        block = plan_ref[step]
        key = plan_ref[groups + step]
        now_ref[...] = near_ref[jnp.minimum(key, near - 1)]

        @pl.when(step >= head)
        def _():
            far_block = far_ref[jnp.clip(key - near, 0, groups - near - 1)]
            now_ref[...] = jnp.where(key >= near, far_block, now_ref[...])

        @pl.when(step >= groups // 2)
        def _():
            twin_block = twin_ref[jnp.maximum(key - groups, 0)]
            now_ref[...] = jnp.where(key >= groups, twin_block, now_ref[...])

        before = jnp.maximum(step - 1, 0)
        rows = read_rows(now_ref[...])
        _, right = exponent_rows(rows)
        right = right_splits(right)
        second = moment_rows(rows)
        first = moment_ref[block]
        left = left_ref[block]
        last_column = partial_ref[:, BLOCK - TILE :]
        by_first = [None] * tiles
        by_second = [None] * tiles
        flying = {}

        def add(sums, index, term):
            sums[index] = term if sums[index] is None else sums[index] + term

        for chunk in range(chunks):
            column, row = divmod(chunk, tiles)
            value = jnp.exp2(dot(left[cut(row)], right[:, cut(column)], 1, 0))
            high = value.astype(BF16)
            flying[chunk] = high, (value - high.astype(F32)).astype(BF16)
            if chunk < DEPTH:
                last_column = settle(before, chunk - DEPTH, last_column)
            if chunk == DEPTH - 1:
                energy = energy + conclude(before, last_column)
            if chunk >= DEPTH:
                column, row = divmod(chunk - DEPTH, tiles)
                high, low = flying.pop(chunk - DEPTH)
                add(by_first, row, first_terms(second[:, cut(column)], high, low))
                add(by_second, column, second_terms(first[:, cut(row)], high, low))
        for place in range(DEPTH):
            high_ref[cut(place)], low_ref[cut(place)] = flying[chunks - DEPTH + place]
        column_ref[...] = second[:, BLOCK - TILE :]
        partial_ref[...] = jnp.concatenate(by_second, axis=1)
        mine_ref[...] = jnp.concatenate(by_first, axis=1)
        back_ref[before] = result_ref[plan_ref[2 * groups + before]]

        @pl.when(step >= 2)
        def _():
            give_back(0, step - 1).start()

        return energy

    for held in (now_ref, high_ref, low_ref, column_ref, partial_ref, mine_ref, local_ref):
        held[...] = jnp.zeros_like(held)
    energy = lax.fori_loop(0, groups, visit, jnp.zeros((1, BLOCK), F32))
    past_ref[...] = now_ref[...]
    last_column = partial_ref[:, BLOCK - TILE :]
    for number in range(-DEPTH, 0):
        last_column = settle(groups - 1, number, last_column)
    energy = energy + conclude(groups - 1, last_column)
    back_ref[groups - 1] = result_ref[plan_ref[3 * groups - 1]]
    give_back(0, groups - 1).start()
    share_ref[0] = jnp.full(share_ref.shape[1:], jnp.sum(energy) * (1.0 / BLOCK), F32)
    each(1, rows_x, lambda r: share_across(r).start())

    def send_last(turn):
        r = 1 + lax.rem(12 * turn, groups - 1)
        back_ref[groups + r] = result_ref[plan_ref[3 * groups + r]]
        give_back(1, r).start()

    each(0, groups // 2, send_last)
    all_across.wait_recv()
    across_ref[my_row] = share_ref[0]
    total = across_ref[0]
    for r in range(1, rows_x):
        total = total + across_ref[r]
    share_ref[1] = total
    each(1, groups, lambda r: share_along(r).start())
    along_ref[me] = total
    each(groups // 2, groups - 1, send_last)
    back_ref[groups] = result_ref[plan_ref[3 * groups]]
    home_ref[0] = back_ref[0]
    home_ref[groups] = back_ref[groups]

    def gather(first, last):
        for start in range(0, width, TILE):

            def add(slot, sums, start=start):
                part = home_ref[slot, :, start : start + TILE]
                wish = asked_ref[lax.rem(slot, groups), 0, slot // groups]
                return tuple(kept + jnp.where(wish == block, part, 0.0) for block, kept in enumerate(sums))

            sums = lax.fori_loop(first, last, add, (jnp.zeros((8, TILE), F32),) * owned)
            for block in range(owned):
                sums_ref[block, :, start : start + TILE] += sums[block]

    sums_ref[...] = jnp.zeros_like(sums_ref)
    all_first.wait_recv()
    gather(0, groups)
    all_along.wait_recv()
    total = lax.fori_loop(1, groups, lambda r, kept: kept + along_ref[r], along_ref[0])
    energy_ref[0, 0] = jnp.max(total)
    all_last.wait_recv()
    gather(groups, 2 * groups)
    for block in range(owned):
        unpack(block)
    for copies in (all_asks, all_near, all_far, all_twin, all_first, all_last, all_across, all_along):
        copies.wait_send()


def partner_order(groups):
    if groups != 32:
        return [(r + 1) // 2 if r % 2 else (groups - r // 2) % groups for r in range(groups)]
    close = [8 * (m // 3 - 1) + 2 * (m % 3 - 1) for m in [4, 5, 6, 7, 8, 0, 1, 2, 3]]
    wide = [16 + 2 * dx for dx in (-1, 0, 1, 2)] + [4 + 8 * dz for dz in (-1, 0, 1)]
    return [(base + core) % groups for base in close + wide for core in (0, 1)]


def shards(features, first_slot, second_owner, second_slot, pair_count):
    owned = features.shape[1] // BLOCK
    entries = first_slot.shape[0]
    groups = lax.axis_size("gy")
    slots = 2 * groups
    near = groups // 2 + max(1, groups // 16)
    me = lax.axis_index("gy")
    owners = second_owner[:, 0]
    order = jnp.arange(entries, dtype=jnp.int32)
    far = jnp.arange(slots, dtype=jnp.int32)
    live = order < pair_count[0]
    factors = jnp.where((owners == me) & (second_slot == first_slot), 1, 2)
    factors = jnp.where(live, factors, 0)
    rank = jnp.sum((owners[:, None] == owners[None, :]) & (order[None, :] < order[:, None]), axis=1)
    ahead = lax.rem(owners - me + groups, groups)
    offsets = jnp.asarray(partner_order(groups), jnp.int32)
    distance = jnp.sum(
        jnp.where(ahead[:, None] == offsets[None, :], jnp.arange(groups, dtype=jnp.int32)[None, :], 0), axis=1
    )
    key = rank.astype(jnp.int32) * groups + distance
    place = jnp.sum(key[None, :] < key[:, None], axis=1).astype(jnp.int32)
    at_step = place[None, :] == order[:, None]
    at_slot = key[None, :] == far[:, None]

    def pick(table, values):
        return jnp.sum(jnp.where(table, values[None, :], 0), axis=1)

    want = pick(at_slot, second_slot + 1) - 1
    serve = pick(at_slot, place - groups) + groups
    plan = jnp.concatenate(
        [pick(at_step, first_slot), pick(at_step, key), serve, want, pick(at_step, factors)]
    ).astype(jnp.int32)
    lane = jnp.arange(128, dtype=jnp.int32)[None, :]
    asked = jnp.where(lane == 0, want[:groups, None], jnp.where(lane == 1, want[groups:, None], 0))

    smem = pl.BlockSpec(memory_space=pltpu.SMEM)
    vmem = pl.BlockSpec(memory_space=pltpu.VMEM)
    gradient, energy = pl.pallas_call(
        pair_kernel,
        out_shape=[
            jax.ShapeDtypeStruct((6, owned * BLOCK), F32),
            jax.ShapeDtypeStruct((1, 1), F32),
        ],
        in_specs=[smem, vmem, vmem],
        out_specs=[vmem, smem],
        scratch_shapes=[
            pltpu.VMEM((owned, 7, BLOCK), F32),
            pltpu.VMEM((owned, BLOCK, 48), BF16),
            pltpu.VMEM((owned, 64, BLOCK), BF16),
            pltpu.VMEM((groups, 1, 128), jnp.int32),
            pltpu.SMEM((groups, 1, 128), jnp.int32),
            pltpu.VMEM((slots, 7, BLOCK), F32),
            pltpu.VMEM((near, 7, BLOCK), F32),
            pltpu.VMEM((groups - near, 7, BLOCK), F32),
            pltpu.VMEM((groups, 7, BLOCK), F32),
            pltpu.VMEM((7, BLOCK), F32),
            pltpu.VMEM((32, BLOCK), F32),
            pltpu.VMEM((groups + 1, 8, BLOCK - BLOCK // 4), F32),
            pltpu.VMEM((slots, 8, BLOCK - BLOCK // 4), F32),
            pltpu.VMEM((slots, 8, BLOCK - BLOCK // 4), F32),
            pltpu.VMEM((2, 8, 128), F32),
            pltpu.VMEM((lax.axis_size("gx"), 8, 128), F32),
            pltpu.VMEM((groups, 8, 128), F32),
            pltpu.VMEM((7, BLOCK), F32),
            pltpu.VMEM((DEPTH * TILE, TILE), BF16),
            pltpu.VMEM((DEPTH * TILE, TILE), BF16),
            pltpu.VMEM((64, TILE), BF16),
            pltpu.VMEM((32, BLOCK), F32),
            pltpu.VMEM((owned, 8, BLOCK), F32),
            pltpu.VMEM((owned, 8, BLOCK - BLOCK // 4), F32),
            pltpu.SemaphoreType.DMA((8,)),
            pltpu.SemaphoreType.DMA((8,)),
            pltpu.SemaphoreType.DMA,
        ],
        compiler_params=pltpu.CompilerParams(
            vmem_limit_bytes=56 * 2**20, collective_id=0, has_side_effects=True
        ),
    )(plan, asked.reshape(groups, 1, 128), features)
    return (gradient, energy.reshape(()))


def solution(mesh):
    return jax.shard_map(
        shards,
        mesh=mesh,
        in_specs=(
            P(None, ("gx", "gy")),
            P(("gx", "gy")),
            P(("gx", "gy"), None),
            P(("gx", "gy")),
            P(("gx", "gy")),
        ),
        out_specs=(P(None, ("gx", "gy")), P()),
        check_vma=False,
    )
```

```python
import jax
import jax.numpy as jnp
from jax import lax
from jax.experimental import pallas as pl
from jax.experimental.pallas import tpu as pltpu
from jax.sharding import PartitionSpec as P

BLOCK = 1024
TILE = 256
DEPTH = 3
LOG2E = 1.4426950408889634
F32 = jnp.float32
BF16 = jnp.bfloat16


def dot(left, right, left_dim, right_dim):
    return lax.dot_general(
        left, right, (((left_dim,), (right_dim,)), ((), ())), preferred_element_type=F32
    )


def split_three(value):
    high = value.astype(BF16).astype(F32)
    rest = value - high
    mid = rest.astype(BF16).astype(F32)
    return high, mid, rest - mid


def select_rows(rows):
    index = lax.broadcasted_iota(jnp.int32, (8, BLOCK), 0)
    tile = jnp.zeros((8, BLOCK), F32)
    for place, row in enumerate(rows):
        tile = jnp.where(index == place, row, tile)
    return tile


def read_rows(block):
    return [block[row : row + 1] for row in range(7)]


def exponent_rows(rows):
    x, y, z = rows[:3]
    norm = (-0.5 * LOG2E) * (x * x + y * y + z * z)
    one = jnp.ones_like(x)
    left = select_rows([LOG2E * x, LOG2E * y, LOG2E * z, one, norm])
    right = select_rows([x, y, z, norm, one])
    return left, right


def left_splits(left):
    high, mid, low = split_three(left)
    return jnp.concatenate([high, high, mid, mid, high, low], axis=0)


def right_splits(right):
    high, mid, low = split_three(right)
    return jnp.concatenate([high, mid, high, mid, low, high], axis=0).astype(BF16)


def normal_products(rows):
    nx, ny, nz = rows[3:6]
    return select_rows([nx, ny, nz, nx, nx, ny]) * select_rows([nx, ny, nz, ny, nz, nz])


def moment_rows(rows):
    x, y, z, w = rows[0], rows[1], rows[2], rows[6]
    base = normal_products(rows) * w
    full = jnp.concatenate([base, base * x, base * y, base * z], axis=0)
    high = full.astype(BF16)
    low = (full - high.astype(F32)).astype(BF16)
    return jnp.concatenate([high, low], axis=0)


def finish(rows, moments, factor):
    x, y, z, nx, ny, nz, w = rows
    index = lax.broadcasted_iota(jnp.int32, (8, BLOCK), 0)
    doubled = normal_products(rows) * jnp.where(index < 3, 1.0, 2.0)
    mass = w * factor
    m0 = moments[0:8]
    sums = [
        jnp.sum(doubled * moments[8 * part : 8 * part + 8], axis=0, keepdims=True) * mass
        for part in range(4)
    ]
    xx, yy, zz, xy, xz, yz = [m0[row : row + 1] for row in range(6)]
    twice = 2.0 * mass
    out = select_rows(
        [
            sums[1] - x * sums[0],
            sums[2] - y * sums[0],
            sums[3] - z * sums[0],
            twice * (nx * xx + ny * xy + nz * xz),
            twice * (nx * xy + ny * yy + nz * yz),
            twice * (nx * xz + ny * yz + nz * zz),
        ]
    )
    return out, sums[0]


def pair_kernel(
    plan_ref, features_ref,
    grad_ref, energy_ref,
    want_ref, block_ref, left_ref, moment_ref, ask_ref, asked_ref, out_ref,
    near_ref, far_ref, twin_ref, now_ref, mine_ref, result_ref, back_ref, home_ref,
    share_ref, across_ref, along_ref, past_ref, high_ref, low_ref, column_ref, partial_ref, local_ref, sums_ref,
    send_sem, recv_sem, local_sem,
):
    groups = want_ref.shape[0]
    rows_x = lax.axis_size("gx")
    owned = block_ref.shape[0]
    near = near_ref.shape[0]
    head = near - groups // 2
    me = lax.axis_index("gy")
    my_row = lax.axis_index("gx")

    def offset(r):
        if groups != 32:
            half, odd = (r + 1) // 2, lax.rem(r, 2)
            return odd * half + (1 - odd) * (groups - half)
        core = lax.rem(r, 2)
        ring = lax.rem(r // 2 + 4, 9)
        close = 8 * (ring // 3) + 2 * lax.rem(ring, 3) - 10 + core
        rest = jnp.maximum(r - 18, 0)
        across_z = 14 + 2 * (rest // 2) + core
        across_x = 8 * (jnp.maximum(rest - 8, 0) // 2) - 4 + core
        beyond, last = r // 18, rest // 8
        return 32 + (1 - beyond) * close + beyond * ((1 - last) * across_z + last * across_x)

    def ahead(r):
        return {"gy": lax.rem(me + offset(r), groups)}

    def behind(r):
        return {"gy": lax.rem(me + 3 * groups - offset(r), groups)}

    def remote(kind, source, target, device):
        return pltpu.make_async_remote_copy(
            src_ref=source, dst_ref=target, send_sem=send_sem.at[kind], recv_sem=recv_sem.at[kind],
            device_id=device, device_id_type=pl.DeviceIdType.MESH,
        )

    def all_of(kind, source, target):
        return remote(kind, source, target, ahead(1))

    def ask(r):
        return remote(0, want_ref.at[r], ask_ref.at[r], ahead(r))

    def fetch_near(r):
        return remote(1, out_ref.at[r], near_ref.at[r], behind(r))

    def fetch_far(r):
        return remote(2, out_ref.at[r], far_ref.at[r - near], behind(r))

    def fetch_twin(r):
        return remote(3, out_ref.at[groups + r], twin_ref.at[r], behind(r))

    def give_back(rank, r):
        return remote(4 + rank, back_ref.at[rank * groups + r], home_ref.at[rank * groups + r], ahead(r))

    def share_across(r):
        return remote(6, share_ref.at[0], across_ref.at[my_row], {"gx": lax.rem(my_row + r, rows_x)})

    def share_along(r):
        return remote(7, share_ref.at[1], along_ref.at[me], ahead(r))

    others = pl.ds(1, groups - 1)
    twins = pl.ds(groups + 1, groups - 1)
    all_asks = all_of(0, want_ref.at[others], ask_ref.at[others])
    all_near = all_of(1, out_ref.at[pl.ds(1, near - 1)], near_ref.at[pl.ds(1, near - 1)])
    all_far = all_of(2, out_ref.at[pl.ds(near, groups - near)], far_ref)
    all_twin = all_of(3, out_ref.at[twins], twin_ref.at[others])
    all_first = all_of(4, back_ref.at[others], home_ref.at[others])
    all_last = all_of(5, back_ref.at[twins], home_ref.at[twins])
    rest_x = pl.ds(0, rows_x - 1)
    all_across = all_of(6, across_ref.at[rest_x], across_ref.at[rest_x])
    all_along = all_of(7, along_ref.at[others], along_ref.at[others])

    def each(first, last, body):
        def step(r, carry):
            body(r)
            return carry

        lax.fori_loop(first, last, step, 0)

    barrier = pltpu.get_barrier_semaphore()

    def greet(r):
        pl.semaphore_signal(barrier, inc=1, device_id=ahead(r), device_id_type=pl.DeviceIdType.MESH)

    def greet_across(r):
        pl.semaphore_signal(
            barrier, inc=1, device_id={"gx": lax.rem(my_row + r, rows_x)}, device_id_type=pl.DeviceIdType.MESH
        )

    each(1, groups, greet)
    each(1, rows_x, greet_across)
    lane = lax.broadcasted_iota(jnp.int32, (1, 128), 1)

    def list_wants(r):
        twin_want = jnp.where(lane == 1, plan_ref[5 * groups + r], 0)
        want_ref[r] = jnp.where(lane == 0, plan_ref[4 * groups + r], twin_want)

    each(0, groups, list_wants)
    for block in range(owned):
        block_ref[block] = features_ref[:, block * BLOCK : (block + 1) * BLOCK]
    pl.semaphore_wait(barrier, groups - 1 + rows_x - 1)

    each(1, groups, lambda r: ask(r).start())
    ask_ref[0] = want_ref[0]
    all_asks.wait_recv()
    fetch_plan = pltpu.make_async_copy(ask_ref, asked_ref, local_sem)
    fetch_plan.start()
    fetch_plan.wait()

    def load_out(place, r):
        out_ref[place * groups + r] = block_ref[jnp.maximum(asked_ref[r, 0, place], 0)]

    def send_near(r):
        load_out(0, r)
        fetch_near(r).start()

    def send_far(r):
        load_out(0, r)
        fetch_far(r).start()

    def send_twin(r):
        load_out(1, r)
        fetch_twin(r).start()

    each(1, near, send_near)
    each(near, groups, send_far)
    each(1, groups, send_twin)
    near_ref[0] = block_ref[jnp.maximum(asked_ref[0, 0, 0], 0)]
    twin_ref[0] = block_ref[jnp.maximum(asked_ref[0, 0, 1], 0)]

    def prepare(block):
        rows = read_rows(block_ref[block])
        left, _ = exponent_rows(rows)
        left_ref[block] = left_splits(left).T.astype(BF16)
        moment_ref[block] = moment_rows(rows)

    each(0, owned, prepare)
    result_ref[groups] = jnp.zeros_like(result_ref[groups])
    all_near.wait_recv()

    tiles = BLOCK // TILE
    width, piece = BLOCK - BLOCK // 4, BLOCK // 8
    chunks = tiles * tiles

    def cut(index):
        return slice(index * TILE, (index + 1) * TILE)

    def first_terms(second, high, low):
        both = dot(second, high, 1, 1)
        return both[0:32] + both[32:64] + dot(second[0:32], low, 1, 1)

    def second_terms(first, high, low):
        both = dot(first, high, 1, 0)
        return both[0:32] + both[32:64] + dot(first[0:32], low, 1, 0)

    def settle(entry, number, last_column):
        place = number + DEPTH
        high, low = high_ref[cut(place)], low_ref[cut(place)]
        rows = cut(tiles + number)
        mine_ref[:, rows] += first_terms(column_ref[...], high, low)
        first = moment_ref[plan_ref[entry], :, rows]
        return last_column + second_terms(first, high, low)

    def pack(entry, out):
        result_ref[entry, 0:6] = out[0:6, :width]
        for part in range(6):
            top, start = 2 * (part % 3), width + (part // 3) * piece
            result_ref[entry, 6:8, part * piece : (part + 1) * piece] = out[top : top + 2, start : start + piece]

    def unpack(block):
        start = block * BLOCK
        local_ref[block, 0:6, :width] += sums_ref[block, 0:6]
        for part in range(6):
            top, place = 2 * (part % 3), width + (part // 3) * piece
            local_ref[block, top : top + 2, place : place + piece] += sums_ref[
                block, 6:8, part * piece : (part + 1) * piece
            ]
        grad_ref[:, start : start + BLOCK] = local_ref[block, 0:6]

    def conclude(entry, last_column):
        moments = jnp.concatenate([partial_ref[:, : BLOCK - TILE], last_column], axis=1)
        factor = plan_ref[6 * groups + entry].astype(F32)
        out, share = finish(read_rows(past_ref[...]), moments, factor)
        pack(entry, out)
        block = plan_ref[entry]
        out, _ = finish(read_rows(block_ref[block]), mine_ref[...], factor)
        for own in range(owned):
            local_ref[own] += jnp.where(block == own, out, 0.0)
        return share

    def visit(step, energy):
        past_ref[...] = now_ref[...]

        @pl.when(step == head)
        def _():
            all_far.wait_recv()

        @pl.when(step == groups // 2)
        def _():
            all_twin.wait_recv()

        block = plan_ref[step]
        key = plan_ref[groups + step]
        now_ref[...] = near_ref[jnp.minimum(key, near - 1)]

        @pl.when(step >= head)
        def _():
            far_block = far_ref[jnp.clip(key - near, 0, groups - near - 1)]
            now_ref[...] = jnp.where(key >= near, far_block, now_ref[...])

        @pl.when(step >= groups // 2)
        def _():
            twin_block = twin_ref[jnp.maximum(key - groups, 0)]
            now_ref[...] = jnp.where(key >= groups, twin_block, now_ref[...])

        before = jnp.maximum(step - 1, 0)
        rows = read_rows(now_ref[...])
        _, right = exponent_rows(rows)
        right = right_splits(right)
        second = moment_rows(rows)
        first = moment_ref[block]
        left = left_ref[block]
        last_column = partial_ref[:, BLOCK - TILE :]
        by_first = [None] * tiles
        by_second = [None] * tiles
        flying = {}

        def add(sums, index, term):
            sums[index] = term if sums[index] is None else sums[index] + term

        for chunk in range(chunks):
            column, row = divmod(chunk, tiles)
            value = jnp.exp2(dot(left[cut(row)], right[:, cut(column)], 1, 0))
            high = value.astype(BF16)
            flying[chunk] = high, (value - high.astype(F32)).astype(BF16)
            if chunk < DEPTH:
                last_column = settle(before, chunk - DEPTH, last_column)
            if chunk == DEPTH - 1:
                energy = energy + conclude(before, last_column)
            if chunk >= DEPTH:
                column, row = divmod(chunk - DEPTH, tiles)
                high, low = flying.pop(chunk - DEPTH)
                add(by_first, row, first_terms(second[:, cut(column)], high, low))
                add(by_second, column, second_terms(first[:, cut(row)], high, low))
        for place in range(DEPTH):
            high_ref[cut(place)], low_ref[cut(place)] = flying[chunks - DEPTH + place]
        column_ref[...] = second[:, BLOCK - TILE :]
        partial_ref[...] = jnp.concatenate(by_second, axis=1)
        mine_ref[...] = jnp.concatenate(by_first, axis=1)
        back_ref[before] = result_ref[plan_ref[2 * groups + before]]

        @pl.when(step >= 2)
        def _():
            give_back(0, step - 1).start()

        return energy

    for held in (now_ref, high_ref, low_ref, column_ref, partial_ref, mine_ref, local_ref):
        held[...] = jnp.zeros_like(held)
    energy = lax.fori_loop(0, groups, visit, jnp.zeros((1, BLOCK), F32))
    past_ref[...] = now_ref[...]
    last_column = partial_ref[:, BLOCK - TILE :]
    for number in range(-DEPTH, 0):
        last_column = settle(groups - 1, number, last_column)
    energy = energy + conclude(groups - 1, last_column)
    back_ref[groups - 1] = result_ref[plan_ref[3 * groups - 1]]
    give_back(0, groups - 1).start()
    share_ref[0] = jnp.full(share_ref.shape[1:], jnp.sum(energy) * (1.0 / BLOCK), F32)
    each(1, rows_x, lambda r: share_across(r).start())

    def send_last(turn):
        r = 1 + lax.rem(12 * turn, groups - 1)
        back_ref[groups + r] = result_ref[plan_ref[3 * groups + r]]
        give_back(1, r).start()

    each(0, groups // 2, send_last)
    all_across.wait_recv()
    across_ref[my_row] = share_ref[0]
    total = across_ref[0]
    for r in range(1, rows_x):
        total = total + across_ref[r]
    share_ref[1] = total
    each(1, groups, lambda r: share_along(r).start())
    along_ref[me] = total
    each(groups // 2, groups - 1, send_last)
    back_ref[groups] = result_ref[plan_ref[3 * groups]]
    home_ref[0] = back_ref[0]
    home_ref[groups] = back_ref[groups]

    def gather(first, last):
        for start in range(0, width, TILE):

            def add(slot, sums, start=start):
                part = home_ref[slot, :, start : start + TILE]
                wish = asked_ref[lax.rem(slot, groups), 0, slot // groups]
                return tuple(kept + jnp.where(wish == block, part, 0.0) for block, kept in enumerate(sums))

            sums = lax.fori_loop(first, last, add, (jnp.zeros((8, TILE), F32),) * owned)
            for block in range(owned):
                sums_ref[block, :, start : start + TILE] += sums[block]

    sums_ref[...] = jnp.zeros_like(sums_ref)
    all_first.wait_recv()
    gather(0, groups)
    all_along.wait_recv()
    total = lax.fori_loop(1, groups, lambda r, kept: kept + along_ref[r], along_ref[0])
    energy_ref[0, 0] = jnp.max(total)
    all_last.wait_recv()
    gather(groups, 2 * groups)
    for block in range(owned):
        unpack(block)
    for copies in (all_asks, all_near, all_far, all_twin, all_first, all_last, all_across, all_along):
        copies.wait_send()


def partner_order(groups):
    if groups != 32:
        return [(r + 1) // 2 if r % 2 else (groups - r // 2) % groups for r in range(groups)]
    close = [8 * (m // 3 - 1) + 2 * (m % 3 - 1) for m in [4, 5, 6, 7, 8, 0, 1, 2, 3]]
    wide = [16 + 2 * dx for dx in (-1, 0, 1, 2)] + [4 + 8 * dz for dz in (-1, 0, 1)]
    return [(base + core) % groups for base in close + wide for core in (0, 1)]


def shards(features, first_slot, second_owner, second_slot, pair_count):
    owned = features.shape[1] // BLOCK
    entries = first_slot.shape[0]
    groups = lax.axis_size("gy")
    slots = 2 * groups
    near = groups // 2 + max(1, groups // 16)
    me = lax.axis_index("gy")
    owners = second_owner[:, 0]
    order = jnp.arange(entries, dtype=jnp.int32)
    far = jnp.arange(slots, dtype=jnp.int32)
    live = order < pair_count[0]
    factors = jnp.where((owners == me) & (second_slot == first_slot), 1, 2)
    factors = jnp.where(live, factors, 0)
    rank = jnp.sum((owners[:, None] == owners[None, :]) & (order[None, :] < order[:, None]), axis=1)
    ahead = lax.rem(owners - me + groups, groups)
    offsets = jnp.asarray(partner_order(groups), jnp.int32)
    distance = jnp.sum(
        jnp.where(ahead[:, None] == offsets[None, :], jnp.arange(groups, dtype=jnp.int32)[None, :], 0), axis=1
    )
    key = rank.astype(jnp.int32) * groups + distance
    place = jnp.sum(key[None, :] < key[:, None], axis=1).astype(jnp.int32)
    at_step = place[None, :] == order[:, None]
    at_slot = key[None, :] == far[:, None]

    def pick(table, values):
        return jnp.sum(jnp.where(table, values[None, :], 0), axis=1)

    want = pick(at_slot, second_slot + 1) - 1
    serve = pick(at_slot, place - groups) + groups
    plan = jnp.concatenate(
        [pick(at_step, first_slot), pick(at_step, key), serve, want, pick(at_step, factors)]
    ).astype(jnp.int32)

    smem = pl.BlockSpec(memory_space=pltpu.SMEM)
    vmem = pl.BlockSpec(memory_space=pltpu.VMEM)
    gradient, energy = pl.pallas_call(
        pair_kernel,
        out_shape=[
            jax.ShapeDtypeStruct((6, owned * BLOCK), F32),
            jax.ShapeDtypeStruct((1, 1), F32),
        ],
        in_specs=[smem, vmem],
        out_specs=[vmem, smem],
        scratch_shapes=[
            pltpu.VMEM((groups, 1, 128), jnp.int32),
            pltpu.VMEM((owned, 7, BLOCK), F32),
            pltpu.VMEM((owned, BLOCK, 48), BF16),
            pltpu.VMEM((owned, 64, BLOCK), BF16),
            pltpu.VMEM((groups, 1, 128), jnp.int32),
            pltpu.SMEM((groups, 1, 128), jnp.int32),
            pltpu.VMEM((slots, 7, BLOCK), F32),
            pltpu.VMEM((near, 7, BLOCK), F32),
            pltpu.VMEM((groups - near, 7, BLOCK), F32),
            pltpu.VMEM((groups, 7, BLOCK), F32),
            pltpu.VMEM((7, BLOCK), F32),
            pltpu.VMEM((32, BLOCK), F32),
            pltpu.VMEM((groups + 1, 8, BLOCK - BLOCK // 4), F32),
            pltpu.VMEM((slots, 8, BLOCK - BLOCK // 4), F32),
            pltpu.VMEM((slots, 8, BLOCK - BLOCK // 4), F32),
            pltpu.VMEM((2, 8, 128), F32),
            pltpu.VMEM((lax.axis_size("gx"), 8, 128), F32),
            pltpu.VMEM((groups, 8, 128), F32),
            pltpu.VMEM((7, BLOCK), F32),
            pltpu.VMEM((DEPTH * TILE, TILE), BF16),
            pltpu.VMEM((DEPTH * TILE, TILE), BF16),
            pltpu.VMEM((64, TILE), BF16),
            pltpu.VMEM((32, BLOCK), F32),
            pltpu.VMEM((owned, 8, BLOCK), F32),
            pltpu.VMEM((owned, 8, BLOCK - BLOCK // 4), F32),
            pltpu.SemaphoreType.DMA((8,)),
            pltpu.SemaphoreType.DMA((8,)),
            pltpu.SemaphoreType.DMA,
        ],
        compiler_params=pltpu.CompilerParams(
            vmem_limit_bytes=56 * 2**20, collective_id=0, has_side_effects=True
        ),
    )(plan, features)
    return (gradient, energy.reshape(()))


def solution(mesh):
    return jax.shard_map(
        shards,
        mesh=mesh,
        in_specs=(
            P(None, ("gx", "gy")),
            P(("gx", "gy")),
            P(("gx", "gy"), None),
            P(("gx", "gy")),
            P(("gx", "gy")),
        ),
        out_specs=(P(None, ("gx", "gy")), P()),
        check_vma=False,
    )
```
